256 devices in a mesh: group: 2 (over y_hi), wide: 128 (over y_lo, z, x, core).
Axes of the slice: x: 4, y: 4 (y_hi: 2, y_lo: 2; y = y_hi * 2 + y_lo), z: 8, core: 2. Of those that a mesh axis runs over, the one named last changes fastest.
Arguments:
- tokens: bfloat16 [16384, 2880], P('wide'), may hold values from -6 to 6
- routes: int32 [16384, 4], P('wide'), may hold values from 0 to 127, all different within a row; in each aligned block of 128 rows (0 to 127, 128 to 255, ...) at most 8 rows name the same one
- router: bfloat16 [2880, 128], replicated, may hold values from -0.109375 to 0.109375
- gate_codes: int32 [128, 960, 1536], P('wide', None, 'group'), may hold values from 0 to 4095
- gate_scales: int32 [128, 90, 1536], P('wide', None, 'group'), may hold values from -9 to -6
- up_codes: int32 [128, 960, 1536], P('wide', None, 'group'), may hold values from 0 to 4095
- up_scales: int32 [128, 90, 1536], P('wide', None, 'group'), may hold values from -9 to -6
- down_codes: int32 [128, 512, 2880], P('wide', 'group'), may hold values from 0 to 4095
- down_scales: int32 [128, 48, 2880], P('wide', 'group'), may hold values from -8 to -5
- norm_gain: float32 [2880], replicated, may hold values from 0.25 to 1.75
- drafter_weight: bfloat16 [1536, 2880], P(('group', 'wide')), may hold values from -0.109375 to 0.109375
Outputs:
- draft_error: bfloat16 [16384, 1536], P('wide', 'group')
- draft_grad: bfloat16 [1536, 2880], P(('group', 'wide'))
The draws below stay inside these ranges and needn't reach their ends.
Inputs may be any that keep to these rules, and one draw needn't show every extreme that they name: `routes`: each token names 4 different experts; among the 128 tokens of one device no expert is named more than 8 times.
All inputs are finite; a program needn't handle non-finite values.
Results may differ from the reference program's by a relative error of at most 0.007.
Values may be sent and summed in bfloat16 or wider, within the bound.
A program may use at most 192 MiB of HBM per device.

```python
import math
import jax
import jax.numpy as jnp
import numpy as np
from jax import lax

D = 2880
FF = 1536
TOP = 4
DRAFT_OUT = 1536
TOK_DEV = 128
EXPERTS = 128
TOKENS = 16384
CAP = 8
N_GROUP = 2
N_WIDE = 128


def plant(array, rng, smallest, high):
    place = [jax.random.randint(jax.random.fold_in(rng, axis), (), 0, length) for axis, length in enumerate(array.shape)]
    longest = array.shape.index(max(array.shape))
    beside = place[:longest] + [(place[longest] + 1) % array.shape[longest]] + place[longest + 1:]
    return array.at[tuple(place)].set(smallest).at[tuple(beside)].set(high)


def level_of(key, extent, cuts, smallest, top_value):
    factor_of, own = 1.0, jax.random.fold_in(key, 6)
    for dim, blocks in cuts:
        heights = jnp.exp(jax.random.uniform(jax.random.fold_in(own, dim), (blocks,), jnp.float32, smallest / len(cuts), top_value / len(cuts)))
        factor_of = factor_of * jnp.repeat(heights, extent[dim] // blocks).reshape([-1 if axis == dim else 1 for axis in range(len(extent))])
    return factor_of


def assign_block(own_key, own, number, rows, amount, top, most, lean):
    order = jax.random.permutation(own_key, amount)
    crowded, ordinary = portions_of(amount, rows * top, most, lean, True), portions_of(amount, rows * top, most, lean, False)
    places = jnp.arange(amount)

    def named(sizes, offset_by):
        used = int((sizes > 0).sum())
        fixed = max(1, used // 4)
        moved = fixed + (places - fixed + offset_by * (used - fixed)) % max(1, amount - fixed)
        return jnp.zeros((amount,), jnp.int32).at[order[jnp.where(places < fixed, places, moved)]].set(jnp.asarray(sizes, jnp.int32))

    sizes = jnp.where(number % 4 == 0, named(crowded, number // 4), named(ordinary, number - number // 4 - 1))
    mixed = jax.random.permutation(jax.random.fold_in(own, 3), amount)
    giver, taker = mixed[0:amount // 2 * 2:2], mixed[1:amount // 2 * 2:2]
    margin = jnp.minimum(sizes[giver] - 1, most - sizes[taker]) // 2
    margin = jnp.where((giver == order[0]) | (taker == order[0]) | (sizes[taker] == 0), 0, jnp.maximum(margin, 0))
    moved = jax.random.randint(jax.random.fold_in(own, 4), (amount // 2,), 0, 1 << 20) % (margin + 1)
    sizes = sizes.at[giver].add(-moved).at[taker].add(moved)
    members = jnp.searchsorted(jnp.cumsum(sizes), jnp.arange(rows * top), side="right").astype(jnp.int32)
    listing = members.reshape(top, rows).T
    listing = listing[jax.random.permutation(jax.random.fold_in(own, 1), rows)]
    offset_by = jax.random.randint(jax.random.fold_in(own, 2), (rows, 1), 0, top)
    return jnp.take_along_axis(listing, (jnp.arange(top)[None, :] + offset_by) % top, axis=1)


def portions_of(number_of, total, most, lean, full):
    weights = [(1 << 20) // math.isqrt(rank ** lean) + 1 for rank in range(1, number_of + 1)]
    largest = most if full else min(most, max(-(-total // number_of), total * weights[0] // sum(weights)))
    least = 1 if total - largest >= number_of - 1 else 0
    counts, surplus = [largest] + [least] * (number_of - 1), total - largest - least * (number_of - 1)
    while surplus > 0:
        movable = [i for i in range(1, number_of) if counts[i] < largest] or [i for i in range(1, number_of) if counts[i] < most]
        mass, budget = sum([weights[i] for i in movable]), surplus
        for i in movable:
            addition = min(most - counts[i], max(1, budget * weights[i] // mass), surplus)
            counts[i] = counts[i] + addition
            surplus = surplus - addition
    return np.array(counts)


def bell_draw(own_key, dims, spread, most, cuts=(), kind=jnp.bfloat16):
    entries = spread * jax.random.normal(own_key, dims, jnp.float32)
    if cuts:
        entries = entries * level_of(own_key, dims, cuts, -0.22, 0.18)
    return jnp.clip(entries, -most, most).astype(kind)


def setup_inputs(seed: int = 0) -> dict:
    key_list = jax.random.split(jax.random.key(seed), 12)
    tokens = bell_draw(key_list[0], (TOKENS, D), 1.0, 6.0, ((0, 128),))
    routes_keys = jax.random.split(jax.random.fold_in(key_list[1], 1), TOKENS // TOK_DEV)
    routes_turns = jax.random.permutation(jax.random.fold_in(key_list[1], 3), TOKENS // TOK_DEV)
    routes = jax.vmap(lambda own, number: assign_block(jax.random.fold_in(key_list[1], 2), own, number, TOK_DEV, EXPERTS, TOP, CAP, 2))(routes_keys, routes_turns).reshape((TOKENS, TOP))
    router = bell_draw(key_list[2], (D, EXPERTS), D ** -0.5, 0.109375)
    gate_codes = plant(jax.random.randint(key_list[3], (EXPERTS, D // 3, FF), 0, 4096), jax.random.fold_in(key_list[3], 1), 0, 4095).astype(jnp.int32)
    gate_scales = plant(jax.random.randint(key_list[4], (EXPERTS, D // 32, FF), -9, -5), jax.random.fold_in(key_list[4], 1), -9, (-5) - 1).astype(jnp.int32)
    up_codes = plant(jax.random.randint(key_list[5], (EXPERTS, D // 3, FF), 0, 4096), jax.random.fold_in(key_list[5], 1), 0, 4095).astype(jnp.int32)
    up_scales = plant(jax.random.randint(key_list[6], (EXPERTS, D // 32, FF), -9, -5), jax.random.fold_in(key_list[6], 1), -9, (-5) - 1).astype(jnp.int32)
    down_codes = plant(jax.random.randint(key_list[7], (EXPERTS, FF // 3, D), 0, 4096), jax.random.fold_in(key_list[7], 1), 0, 4095).astype(jnp.int32)
    down_scales = plant(jax.random.randint(key_list[8], (EXPERTS, FF // 32, D), -8, -4), jax.random.fold_in(key_list[8], 1), -8, (-4) - 1).astype(jnp.int32)
    norm_gain = jnp.clip(1.0 + 0.15 * jax.random.normal(key_list[9], (D,), jnp.float32), 0.25, 1.75)
    drafter_weight = bell_draw(key_list[10], (DRAFT_OUT, D), D ** -0.5, 0.109375, ((0, 256),))
    return dict(tokens=tokens, routes=routes, router=router, gate_codes=gate_codes, gate_scales=gate_scales, up_codes=up_codes, up_scales=up_scales, down_codes=down_codes, down_scales=down_scales, norm_gain=norm_gain, drafter_weight=drafter_weight)


def dequantize(packed, exponents):
    shifts = 4 * jnp.arange(3, dtype=jnp.int32)
    nibble = packed[:, None, :] >> shifts[None, :, None] & 15
    magnitude = nibble & 7
    level = magnitude.astype(jnp.bfloat16)
    values = jnp.where(magnitude < 4, level * 0.5, jnp.where(magnitude == 7, 6.0, level - 2.0)).astype(jnp.bfloat16)
    values = jnp.where(nibble >= 8, -values, values)
    row_count = packed.shape[0] * 3
    values = values.reshape(row_count, packed.shape[1])
    multiplier = jnp.repeat(jnp.exp2(exponents.astype(jnp.float32)).astype(jnp.bfloat16), 32, axis=0)
    return values * multiplier

def reference(tokens, routes, router, gate_codes, gate_scales, up_codes, up_scales, down_codes, down_scales, norm_gain, drafter_weight):
    flat_routes = routes.reshape(-1)
    limit = N_WIDE * CAP
    half_units = FF // N_GROUP

    def one_expert(expert_id, feature):
        matches = flat_routes == expert_id
        positions = jnp.nonzero(matches, size=limit, fill_value=0)[0].astype(jnp.int32)
        matched = jnp.sum(matches.astype(jnp.int32))
        valid = (jnp.arange(limit, dtype=jnp.int32) < matched).astype(jnp.float32)
        token_ids = positions // TOP
        inputs = tokens[token_ids]
        logit = jnp.dot(inputs, router[:, expert_id], preferred_element_type=jnp.float32)
        weight = jax.nn.sigmoid(logit) * valid
        gate_w = dequantize(gate_codes[expert_id], gate_scales[expert_id])
        up_w = dequantize(up_codes[expert_id], up_scales[expert_id])
        down_w = dequantize(down_codes[expert_id], down_scales[expert_id])
        summed = jnp.zeros((limit, D), jnp.float32)
        for part in range(N_GROUP):
            lower = part * half_units
            gate_act = jnp.dot(inputs, gate_w[:, lower:lower + half_units], preferred_element_type=jnp.float32)
            up_act = jnp.dot(inputs, up_w[:, lower:lower + half_units], preferred_element_type=jnp.float32)
            hidden = (jax.nn.silu(gate_act) * up_act).astype(jnp.bfloat16)
            summed = summed + jnp.dot(hidden, down_w[lower:lower + half_units, :], preferred_element_type=jnp.float32)
        rounded = lax.optimization_barrier(summed.astype(jnp.bfloat16)).astype(jnp.float32)
        return feature.at[token_ids].add(weight[:, None] * rounded)
    feature = lax.fori_loop(0, EXPERTS, one_expert, jnp.zeros((TOKENS, D), jnp.float32))
    feature_b = lax.optimization_barrier(feature.astype(jnp.bfloat16)).astype(jnp.float32)
    mean_square = lax.optimization_barrier(jnp.mean(feature_b * feature_b, axis=1, keepdims=True))
    normed = (feature_b * lax.rsqrt(mean_square + 1e-05) * norm_gain[None, :]).astype(jnp.bfloat16)
    predicted = lax.dot_general(normed, drafter_weight, (((1,), (1,)), ((), ())), preferred_element_type=jnp.float32)
    target = jnp.concatenate([normed[1:, :DRAFT_OUT], jnp.zeros((1, DRAFT_OUT), jnp.bfloat16)], axis=0)
    inside = jnp.arange(TOKENS, dtype=jnp.int32) < TOKENS - 1
    draft_error = jnp.where(inside[:, None], predicted - target.astype(jnp.float32), 0.0).astype(jnp.bfloat16)
    grad_scale = 1.0 / math.sqrt(TOKENS)
    draft_grad = lax.dot_general(draft_error, normed, (((0,), (0,)), ((), ())), preferred_element_type=jnp.float32) * grad_scale
    return (draft_error, draft_grad.astype(jnp.bfloat16))
```

```python
import functools
import math

import jax
import jax.numpy as jnp
from jax import lax
from jax.experimental import pallas as pl
from jax.experimental.pallas import tpu as pltpu
from jax.sharding import PartitionSpec as P

MESH = pl.DeviceIdType.MESH
F32 = jnp.float32
BF16 = jnp.bfloat16

D = 2880
TOK = 128
NZ = 8
PLANE = 16
SLOT = 8
SLABS = TOK // SLOT
UNITS = 768
WORDS = 960
BLOCKS = SLABS + 1
META = 6


def place():
    group, wide = lax.axis_index("group"), lax.axis_index("wide")
    y, z, x, c = wide // 64, (wide // 8) % 8, (wide // 2) % 4, wide % 2
    return group, wide, y, z, x, c


def wide_of(y, z, x, c):
    return y * 64 + z * 8 + x * 2 + c


def plane_wide(p, z):
    return (p // 8) * 64 + z * 8 + p % 8


def iota(shape, dim, kind=jnp.int32):
    return lax.broadcasted_iota(jnp.int32, shape, dim).astype(kind)


def dot(a, b):
    return jnp.dot(a, b, preferred_element_type=F32)


def remote(src, dst, send, recv, device):
    return pltpu.make_async_remote_copy(
        src_ref=src, dst_ref=dst, send_sem=send, recv_sem=recv, device_id=device, device_id_type=MESH
    )


def spread(tokens):
    parts = []
    for start, length in [(384 * b, 384) for b in range(7)] + [(2688, 192)]:
        third = length // 3
        row = iota((length, length), 0)
        column = iota((length, length), 1)
        order = (row == 3 * (column % third) + column // third).astype(F32).astype(BF16)
        parts.append(dot(tokens[:, start : start + length], order).astype(BF16))
    return parts


def prep_kernel(tokens_ref, routes_ref, router_ref, weight_ref, out_ref):
    tokens = tokens_ref[...]
    logits = dot(tokens, router_ref[...])
    weight = jax.nn.sigmoid(logits).T
    column = 0
    for part in spread(tokens):
        width = part.shape[1]
        out_ref[0:SLABS, :, column : column + width] = part.astype(F32).reshape(SLABS, SLOT, width).astype(BF16)
        column += width
    out_ref[SLABS, :, :] = weight_ref[...]
    experts = iota((TOK, TOK), 0)
    routes, high, low = [], [], []
    for k in range(4):
        route = routes_ref[k : k + 1, :]
        chosen = jnp.sum(jnp.where(experts == route, weight, 0.0), axis=0, keepdims=True)
        top = chosen.astype(BF16).astype(F32)
        routes.append(route.astype(F32))
        high.append(top)
        low.append(chosen - top)
    line = jnp.concatenate(routes + high + low, axis=1)
    slab = weight_ref[:, 0 : 12 * TOK].astype(F32)
    row = iota((SLOT, 12 * TOK), 0)
    out_ref[SLABS, :, 0 : 12 * TOK] = jnp.where(row == META, line, slab).astype(BF16)


def level(nibble):
    m = nibble & 7
    twice = m + jnp.maximum(m - 4, 0) + 2 * jnp.maximum(m - 6, 0)
    return twice.astype(F32)


def unpack(words, j, scales):
    nibble = (words >> (4 * j)) & 15
    half = jnp.exp2((scales - 1).astype(F32))
    return level(nibble) * jnp.where(nibble >= 8, -half, half)


def scale_rows(ref, q, j, width):
    r = iota((32, width), 0)
    block = (3 * r + j) // 32
    rows = [ref[pl.ds(3 * q + n, 1), :] for n in range(3)]
    return jnp.where(block == 0, rows[0], jnp.where(block == 1, rows[1], rows[2]))


def dequant_in(codes, scales, out, q, base, third):
    words = codes[pl.ds(pl.multiple_of(32 * q, 32), 32), :]
    for j in range(3):
        values = unpack(words, j, scale_rows(scales, q, j, words.shape[1]))
        out[pl.ds(pl.multiple_of(base + third * j, 32), 32), :] = values.astype(BF16)


def dequant_wide(codes, scales, out, first, last):
    def step(q, carry):
        dequant_in(codes, scales, out, q, (q // 4) * 384 + (q % 4) * 32, 128)
        return carry

    lax.fori_loop(first, min(last, 28), step, 0)
    for q in range(28, last):
        dequant_in(codes, scales, out, q, 2688 + (q - 28) * 32, 64)


def dispatch_kernel(
    blk, gc, gs, uc, us, dc, ds, xr, wg, wu, wd, comb, wz,
    agb, snd, gcv, gsv, ucv, usv, dcv, dsv, code_sem, zsend, zrecv, psend, precv, loc,
):
    group, wide, y, z, x, c = place()
    p_me = y * 8 + x * 2 + c
    right = (group, wide_of(y, (z + 1) % 8, x, c))
    left = (group, wide_of(y, (z + 7) % 8, x, c))

    barrier = pltpu.get_barrier_semaphore()
    for neighbour in (left, right):
        pl.semaphore_signal(barrier, inc=1, device_id=neighbour, device_id_type=MESH)

    def greet(j, carry):
        p = (p_me + j) % PLANE
        pl.semaphore_signal(barrier, inc=1, device_id=(group, plane_wide(p, z)), device_id_type=MESH)
        return carry

    lax.fori_loop(1, PLANE, greet, 0)

    def greet_other(j, carry):
        p = (1 - y) * 8 + j
        pl.semaphore_signal(barrier, inc=1, device_id=(1 - group, plane_wide(p, z)), device_id_type=MESH)
        return carry

    lax.fori_loop(0, 8, greet_other, 0)

    code_copies = [
        pltpu.make_async_copy(a, b, code_sem.at[n])
        for n, (a, b) in enumerate([(gc, gcv), (gs, gsv), (uc, ucv), (us, usv), (dc, dcv), (ds, dsv)])
    ]
    for copy in code_copies:
        copy.start()
    pl.semaphore_wait(barrier, 25)

    sigma = 1 - 2 * c
    sends = []

    def forward(source, s, device, n):
        copy = remote(source, agb.at[s], zsend.at[n], zrecv.at[n], device)
        copy.start()
        sends.append(copy)

    def arrived(s, n):
        remote(blk, agb.at[s], zsend.at[n], zrecv.at[n], right).wait_recv()

    upper = (iota((TOK, TOK), 0) < iota((TOK, TOK), 1)).astype(F32).astype(BF16)
    p_rows = iota((PLANE, 1), 0)
    experts = ((p_rows // 8) * 64 + z * 8 + p_rows % 8).astype(F32)

    def relay(source, s):
        meta = source[SLABS, :, 0 : 12 * TOK].astype(F32)[META : META + 1, :]
        named = jnp.zeros((PLANE, TOK), F32)
        weight = jnp.zeros((PLANE, TOK), F32)
        for k in range(4):
            hit = (experts == meta[:, k * TOK : (k + 1) * TOK]).astype(F32)
            value = meta[:, (4 + k) * TOK : (5 + k) * TOK] + meta[:, (8 + k) * TOK : (9 + k) * TOK]
            named = named + hit
            weight = weight + hit * value
        rank = dot(named.astype(BF16), upper)
        slot = iota((PLANE, SLOT, TOK), 1, F32)
        pick = jnp.where(rank[:, None, :] == slot, named[:, None, :], 0.0)
        weighted = (pick * weight[:, None, :]).reshape(TOK, TOK).T
        top = weighted.astype(BF16)
        comb[s, 0] = top
        comb[s, 1] = (weighted - top.astype(F32)).astype(BF16)
        rows = dot(pick.reshape(TOK, TOK).astype(BF16), source[0:SLABS].reshape(TOK, D))
        snd[s] = rows.reshape(PLANE, SLOT, D).astype(BF16)
        wz[s] = source[SLABS]
        pltpu.make_async_copy(snd.at[s, p_me], xr.at[s, p_me], loc.at[s]).start()

        def send(j, carry):
            p = (p_me + j) % PLANE
            across = ((p // 8 + y) % 2) * (s % 2)
            remote(
                snd.at[s, p], xr.at[s, p_me], psend.at[s], precv.at[s],
                ((group + across) % 2, plane_wide(p, z)),
            ).start()
            return carry

        lax.fori_loop(1, PLANE, send, 0)

    forward(blk, z, right, 0)
    forward(blk, z, left, 1)
    relay(blk, z)
    code_copies[0].wait()
    code_copies[1].wait()
    dequant_wide(gcv, gsv, wg, 0, 8)
    for k in (1, 2, 3):
        back, ahead = (z + 8 - k) % 8, (z + k) % 8
        arrived(back, 2 * k - 2)
        if k < 3:
            forward(agb.at[back], back, right, 2 * k)
        arrived(ahead, 2 * k - 1)
        if k < 3:
            forward(agb.at[ahead], ahead, left, 2 * k + 1)
        else:
            far = (z + 8 - 3 * sigma) % 8
            forward(agb.at[far], far, (group, wide_of(y, (z + 8 + sigma) % 8, x, c)), 6)
        relay(agb.at[back], back)
        relay(agb.at[ahead], ahead)
        if k == 1:
            dequant_wide(gcv, gsv, wg, 8, 30)
        elif k == 2:
            code_copies[2].wait()
            code_copies[3].wait()
            dequant_wide(ucv, usv, wu, 0, 30)
        else:
            code_copies[4].wait()
            code_copies[5].wait()

            def down_all(q, carry):
                words = dcv[pl.ds(pl.multiple_of(32 * q, 32), 32), :]
                for j in range(3):
                    values = unpack(words, j, scale_rows(dsv, q, j, D))
                    wd[pl.ds(pl.multiple_of(256 * j + 32 * q, 32), 32), :] = values.astype(BF16)
                return carry

            lax.fori_loop(0, 8, down_all, 0)
    opposite = (z + 4) % 8
    arrived(opposite, 6)
    relay(agb.at[opposite], opposite)
    for copy in sends:
        copy.wait_send()
    for s in range(NZ):
        pltpu.make_async_copy(snd.at[0, 0], xr.at[0, 0], loc.at[s]).wait()
        whole = remote(snd.at[s, pl.ds(0, 15)], xr.at[s, pl.ds(0, 15)], psend.at[s], precv.at[s], right)
        whole.wait_send()
        whole.wait_recv()


def expert_kernel(
    xr, wg, wu, wd, comb, wz, gain, normed_ref, wall,
    hid, snd, ret, maj, mnr, shr, xch, loc, wloc, psend, precv, rsend, rrecv, xsem, wsend, wrecv,
):
    group, wide, y, z, x, c = place()
    p_me = y * 8 + x * 2 + c
    other = (1 - group, wide)
    core = (group, wide_of(y, z, x, 1 - c))
    sigma = 1 - 2 * c
    ahead = (group, wide_of(y, (z + 8 + sigma) % 8, x, c))
    behind = (group, wide_of(y, (z + 8 - sigma) % 8, x, c))

    barrier = pltpu.get_barrier_semaphore()
    for neighbour in (ahead, behind, other):
        pl.semaphore_signal(barrier, inc=1, device_id=neighbour, device_id_type=MESH)

    def greet(j, carry):
        p = (p_me + j) % PLANE
        pl.semaphore_signal(barrier, inc=1, device_id=(group, plane_wide(p, z)), device_id_type=MESH)
        return carry

    lax.fori_loop(1, PLANE, greet, 0)

    pl.semaphore_wait(barrier, 18)

    keep = pltpu.make_async_copy(wz, wall.at[c, y, x], wloc)
    keep.start()

    def share_x(j, carry):
        remote(wz, wall.at[c, y, x], wsend.at[0], wrecv.at[0], (group, wide_of(y, z, (x + j) % 4, c))).start()
        return carry

    lax.fori_loop(1, 4, share_x, 0)
    share_y = remote(wall.at[c, y], wall.at[c, y], wsend.at[1], wrecv.at[1], (group, wide_of(1 - y, z, x, c)))
    share_c = remote(wall.at[c], wall.at[c], wsend.at[2], wrecv.at[2], core)

    def hidden(n, carry):
        inputs = xr[pl.ds(2 * n, 2)].reshape(256, D)
        gate = dot(inputs, wg[...])
        up = dot(inputs, wu[...])
        act = (jax.nn.silu(gate) * up).astype(BF16)
        row = iota((UNITS, UNITS), 0)
        column = iota((UNITS, UNITS), 1)
        order = (row == 3 * (column % 256) + column // 256).astype(F32).astype(BF16)
        hid[pl.ds(pl.multiple_of(256 * n, 256), 256), :] = dot(act, order).astype(BF16)
        return carry

    lax.fori_loop(0, 4, hidden, 0)

    def source(d):
        return (z + 8 + d * sigma) % 8

    def down(d):
        s = source(d)
        rows = dot(hid[pl.ds(pl.multiple_of(TOK * s, TOK), TOK), :], wd[...])
        snd[s] = rows.reshape(PLANE, SLOT, D).astype(BF16)
        pltpu.make_async_copy(snd.at[s, p_me], ret.at[s, p_me], loc.at[s]).start()

        def send(j, carry):
            p = (p_me + j) % PLANE
            remote(
                snd.at[s, p], ret.at[s, p_me], psend.at[s], precv.at[s], (group, plane_wide(p, z))
            ).start()
            return carry

        lax.fori_loop(1, PLANE, send, 0)

    def combined(d):
        s = source(d)
        pltpu.make_async_copy(snd.at[s, p_me], ret.at[s, p_me], loc.at[s]).wait()
        remote(
            snd.at[s, pl.ds(0, 15)], ret.at[s, pl.ds(0, 15)], psend.at[s], precv.at[s], core
        ).wait_recv()
        rows = ret[s].reshape(TOK, D)
        return dot(comb[s, 0], rows) + dot(comb[s, 1], rows)

    sends = []

    def hop(buffer, k, device, n):
        copy = remote(buffer.at[k], buffer.at[k - 1], rsend.at[n, k], rrecv.at[n, k - 1], device)
        copy.start()
        sends.append(copy)

    def landed(buffer, k, n):
        remote(buffer.at[k], buffer.at[k], rsend.at[n, k], rrecv.at[n, k], ahead).wait_recv()

    down(4)
    down(3)
    down(-3)
    maj[4] = combined(4).astype(BF16)
    hop(maj, 4, ahead, 0)
    down(2)
    down(-2)
    mnr[3] = combined(-3).astype(BF16)
    hop(mnr, 3, behind, 1)
    part = combined(3)
    landed(maj, 3, 0)
    maj[3] = (maj[3].astype(F32) + part).astype(BF16)
    hop(maj, 3, ahead, 0)
    keep.wait()
    three = remote(
        wall.at[c, y, pl.ds(0, 3)], wall.at[c, y, pl.ds(0, 3)], wsend.at[0], wrecv.at[0], core
    )
    three.wait_recv()
    share_y.start()
    for k in (2, 1):
        if k == 2:
            down(1)
            down(-1)
            down(0)
        part = combined(-k)
        landed(mnr, k, 1)
        mnr[k] = (mnr[k].astype(F32) + part).astype(BF16)
        hop(mnr, k, behind, 1)
        part = combined(k)
        landed(maj, k, 0)
        maj[k] = (maj[k].astype(F32) + part).astype(BF16)
        hop(maj, k, ahead, 0)
    part = combined(0)
    share_y.wait_recv()
    share_c.start()
    landed(mnr, 0, 1)
    part = part + mnr[0].astype(F32)
    landed(maj, 0, 0)
    part = part + maj[0].astype(F32)
    shr[...] = part.astype(BF16)
    swap = remote(shr, xch, xsem.at[0], xsem.at[1], other)
    swap.start()
    swap.wait()
    feature = (shr[...].astype(F32) + xch[...].astype(F32)).astype(BF16).astype(F32)
    mean_square = jnp.sum(feature * feature, axis=1, keepdims=True) / D
    normed_ref[...] = (feature * lax.rsqrt(mean_square + 1e-05) * gain[...]).astype(BF16)
    for copy in sends:
        copy.wait_send()
    for s in range(NZ):
        remote(
            snd.at[s, pl.ds(0, 15)], ret.at[s, pl.ds(0, 15)], psend.at[s], precv.at[s], core
        ).wait_send()
    three.wait_send()
    share_y.wait_send()
    share_c.wait()


def drafter_order(shape, row_dim, padded):
    feature = iota(shape, row_dim)
    q = iota(shape, 1 - row_dim)
    if padded:
        c, y, x, z, i = q // 512, (q // 256) % 2, (q // 64) % 4, (q // 8) % 8, q % 8
        own = y * 384 + z * 48 + x * 12 + c * 6 + i
        return ((feature == own) & (i < 6)).astype(F32).astype(BF16)
    c, z, y, x, i = q // 384, (q // 48) % 8, (q // 24) % 2, (q // 6) % 4, q % 6
    own = y * 384 + z * 48 + x * 12 + c * 6 + i
    return (feature == own).astype(F32).astype(BF16)


def drafter_kernel(
    grad_scale, normed, wall, error_ref, grad_ref,
    nall, first, err, eall, gsum, maj, mnr, slab, fin, fsem, nsem, esem, rsend, rrecv, psend, precv, loc,
):
    group, wide, y, z, x, c = place()
    yx = y * 4 + x
    core = (group, wide_of(y, z, x, 1 - c))
    before = (group, (wide + 127) % 128)
    after = (group, (wide + 1) % 128)
    sigma = 1 - 2 * c
    ahead = (group, wide_of(y, (z + 8 + sigma) % 8, x, c))
    behind = (group, wide_of(y, (z + 8 - sigma) % 8, x, c))

    def peer(j):
        other = (yx + j) % 8
        return (group, wide_of(other // 4, z, other % 4, c))

    barrier = pltpu.get_barrier_semaphore()
    for neighbour in (ahead, behind, core, before, after):
        pl.semaphore_signal(barrier, inc=1, device_id=neighbour, device_id_type=MESH)

    def greet(j, carry):
        pl.semaphore_signal(barrier, inc=1, device_id=peer(j), device_id_type=MESH)
        return carry

    lax.fori_loop(1, 8, greet, 0)
    pl.semaphore_wait(barrier, 12)

    follow = remote(normed.at[pl.ds(0, 16)], first, fsem.at[0], fsem.at[1], before)
    follow.start()
    keep = pltpu.make_async_copy(normed, nall.at[c], loc.at[0])
    keep.start()
    swap = remote(normed, nall.at[c], nsem.at[0], nsem.at[1], core)
    swap.start()

    predicted = lax.dot_general(
        normed[...], wall[...].reshape(1024, D), (((1,), (1,)), ((), ())), preferred_element_type=F32
    )
    lanes = pl.ds(pl.multiple_of(group * UNITS, 128), UNITS)
    own = normed[:, lanes].astype(F32)
    follow.wait()
    row = iota((TOK, 1), 0)
    nearest = pltpu.roll(own, TOK - 1, 0)
    target = jnp.where(row == TOK - 1, first[:, lanes].astype(F32)[0:1, :], nearest).astype(BF16)
    target = dot(target, drafter_order((UNITS, 1024), 0, True))
    inside = (wide * TOK + row) < 128 * TOK - 1
    residual = jnp.where(inside, predicted - target, 0.0).astype(BF16)
    residual = dot(residual, drafter_order((1024, UNITS), 1, True)).astype(BF16)
    error_ref[...] = residual
    ordered = dot(residual, drafter_order((UNITS, UNITS), 0, False)).astype(BF16)
    err[0] = ordered[:, 0:384]
    err[1] = ordered[:, 384:768]
    keep_err = pltpu.make_async_copy(err.at[c], eall.at[c], loc.at[1])
    keep_err.start()
    swap_err = remote(err.at[1 - c], eall.at[c], esem.at[0], esem.at[1], core)
    swap_err.start()
    keep.wait()
    swap.wait()
    keep_err.wait()
    swap_err.wait()
    factors = eall[...].reshape(256, 384).astype(F32).T.astype(BF16)
    gsum[...] = dot(factors, nall[...].reshape(256, D)) * grad_scale

    def own_part(d):
        s = (z + 8 + d * sigma) % 8
        return gsum[pl.ds(pl.multiple_of(48 * s, 16), 48), :]

    sends = []

    def hop(buffer, k, device, n):
        copy = remote(buffer.at[k], buffer.at[k - 1], rsend.at[n, k], rrecv.at[n, k - 1], device)
        copy.start()
        sends.append(copy)

    def landed(buffer, k, n):
        remote(buffer.at[k], buffer.at[k], rsend.at[n, k], rrecv.at[n, k], ahead).wait_recv()

    maj[4] = own_part(4).astype(BF16)
    hop(maj, 4, ahead, 0)
    mnr[3] = own_part(-3).astype(BF16)
    hop(mnr, 3, behind, 1)
    for k in (3, 2, 1):
        landed(maj, k, 0)
        maj[k] = (maj[k].astype(F32) + own_part(k)).astype(BF16)
        hop(maj, k, ahead, 0)
        if k < 3:
            landed(mnr, k, 1)
            mnr[k] = (mnr[k].astype(F32) + own_part(-k)).astype(BF16)
            hop(mnr, k, behind, 1)
    landed(mnr, 0, 1)
    landed(maj, 0, 0)
    total = (own_part(0) + mnr[0].astype(F32) + maj[0].astype(F32)).astype(BF16)
    q = iota((64, 48), 0)
    expand = ((q // 8) * 6 + q % 8 == iota((64, 48), 1)) & (q % 8 < 6)
    slab[...] = dot(expand.astype(F32).astype(BF16), total).reshape(8, 8, D).astype(BF16)
    keep_fin = pltpu.make_async_copy(slab.at[yx], fin.at[yx], loc.at[2])
    keep_fin.start()

    def send(j, carry):
        remote(slab.at[(yx + j) % 8], fin.at[yx], psend, precv, peer(j)).start()
        return carry

    lax.fori_loop(1, 8, send, 0)
    keep_fin.wait()
    whole = remote(slab.at[pl.ds(0, 7)], fin.at[pl.ds(0, 7)], psend, precv, core)
    whole.wait_recv()
    gradient = jnp.sum(fin[...].astype(F32), axis=0)
    grad_ref[...] = gradient.astype(BF16)
    whole.wait_send()
    for copy in sends:
        copy.wait_send()


def params(number=None):
    if number is None:
        return pltpu.CompilerParams(vmem_limit_bytes=58 << 20)
    return pltpu.CompilerParams(vmem_limit_bytes=58 << 20, collective_id=number, has_side_effects=True)


VM = pl.BlockSpec(memory_space=pltpu.VMEM)
ANY = pl.BlockSpec(memory_space=pl.ANY)


def out(shape, kind=BF16):
    return jax.ShapeDtypeStruct(shape, kind)


def shards(
    tokens, routes, router, gate_codes, gate_scales, up_codes, up_scales, down_codes, down_scales, norm_gain,
    drafter_weight,
):
    dma = pltpu.SemaphoreType.DMA
    padded = jnp.pad(drafter_weight, ((0, 2), (0, 0)))
    block = pl.pallas_call(
        prep_kernel, out_shape=out((BLOCKS, SLOT, D)), in_specs=[VM] * 4, out_specs=VM,
        compiler_params=params(), name="prep",
    )(tokens, routes.T, router, padded)
    frame = (NZ, PLANE, SLOT, D)
    xr, wg, wu, wd, comb, wz = pl.pallas_call(
        dispatch_kernel,
        out_shape=(
            out(frame), out((D, UNITS)), out((D, UNITS)), out((UNITS, D)), out((NZ, 2, TOK, TOK)), out((NZ, SLOT, D)),
        ),
        in_specs=[VM] + [ANY] * 6,
        out_specs=(VM,) * 6,
        scratch_shapes=[
            pltpu.VMEM((NZ, BLOCKS, SLOT, D), BF16),
            pltpu.VMEM(frame, BF16),
            pltpu.VMEM((WORDS, UNITS), jnp.int32),
            pltpu.VMEM((90, UNITS), jnp.int32),
            pltpu.VMEM((WORDS, UNITS), jnp.int32),
            pltpu.VMEM((90, UNITS), jnp.int32),
            pltpu.VMEM((256, D), jnp.int32),
            pltpu.VMEM((24, D), jnp.int32),
            dma((6,)), dma((7,)), dma((7,)), dma((NZ,)), dma((NZ,)), dma((NZ,)),
        ],
        compiler_params=params(1),
        name="dispatch",
    )(
        block, gate_codes[0], gate_scales[0], up_codes[0], up_scales[0], down_codes[0], down_scales[0],
    )
    normed, wall = pl.pallas_call(
        expert_kernel,
        out_shape=(out((TOK, D)), out((2, 2, 4, NZ, SLOT, D))),
        in_specs=[VM] * 7,
        out_specs=(VM, VM),
        scratch_shapes=[
            pltpu.VMEM((1024, UNITS), BF16),
            pltpu.VMEM(frame, BF16),
            pltpu.VMEM(frame, BF16),
            pltpu.VMEM((5, TOK, D), BF16),
            pltpu.VMEM((4, TOK, D), BF16),
            pltpu.VMEM((TOK, D), BF16),
            pltpu.VMEM((TOK, D), BF16),
            dma((NZ,)), dma, dma((NZ,)), dma((NZ,)), dma((2, 5)), dma((2, 5)), dma((2,)), dma((3,)), dma((3,)),
        ],
        compiler_params=params(2),
        name="experts",
    )(xr, wg, wu, wd, comb, wz, norm_gain[None, :])
    grad_scale = 1.0 / math.sqrt(TOK * lax.axis_size("wide"))
    error, gradient = pl.pallas_call(
        functools.partial(drafter_kernel, grad_scale),
        out_shape=(out((TOK, UNITS)), out((SLOT, D))),
        in_specs=[VM] * 2,
        out_specs=(VM, VM),
        scratch_shapes=[
            pltpu.VMEM((2, TOK, D), BF16),
            pltpu.VMEM((16, D), BF16),
            pltpu.VMEM((2, TOK, 384), BF16),
            pltpu.VMEM((2, TOK, 384), BF16),
            pltpu.VMEM((384, D), F32),
            pltpu.VMEM((5, 48, D), BF16),
            pltpu.VMEM((4, 48, D), BF16),
            pltpu.VMEM((8, SLOT, D), BF16),
            pltpu.VMEM((8, SLOT, D), BF16),
            dma((2,)), dma((2,)), dma((2,)), dma((2, 5)), dma((2, 5)), dma, dma, dma((3,)),
        ],
        compiler_params=params(3),
        name="drafter",
    )(normed, wall)
    return (error, gradient[:6])


def solution(mesh):
    placed = (
        P("wide", None),
        P("wide", None),
        P(),
        P("wide", None, "group"),
        P("wide", None, "group"),
        P("wide", None, "group"),
        P("wide", None, "group"),
        P("wide", "group", None),
        P("wide", "group", None),
        P(),
        P(("group", "wide"), None),
    )
    return jax.shard_map(
        shards,
        mesh=mesh,
        in_specs=placed,
        out_specs=(P("wide", "group"), P(("group", "wide"), None)),
        check_vma=False,
    )
```

```python
import functools
import math

import jax
import jax.numpy as jnp
from jax import lax
from jax.experimental import pallas as pl
from jax.experimental.pallas import tpu as pltpu
from jax.sharding import PartitionSpec as P

MESH = pl.DeviceIdType.MESH
F32 = jnp.float32
BF16 = jnp.bfloat16

D = 2880
TOK = 128
NZ = 8
PLANE = 16
SLOT = 8
SLABS = TOK // SLOT
UNITS = 768
WORDS = 960
BLOCKS = SLABS + 1
META = 6


def place():
    group, wide = lax.axis_index("group"), lax.axis_index("wide")
    y, z, x, c = wide // 64, (wide // 8) % 8, (wide // 2) % 4, wide % 2
    return group, wide, y, z, x, c


def wide_of(y, z, x, c):
    return y * 64 + z * 8 + x * 2 + c


def plane_wide(p, z):
    return (p // 8) * 64 + z * 8 + p % 8


def iota(shape, dim, kind=jnp.int32):
    return lax.broadcasted_iota(jnp.int32, shape, dim).astype(kind)


def dot(a, b):
    return jnp.dot(a, b, preferred_element_type=F32)


def dot_first(a, b):
    return lax.dot_general(a, b, (((0,), (0,)), ((), ())), preferred_element_type=F32)


def remote(src, dst, send, recv, device):
    return pltpu.make_async_remote_copy(
        src_ref=src, dst_ref=dst, send_sem=send, recv_sem=recv, device_id=device, device_id_type=MESH
    )


def spread(columns):
    parts = []
    for start, length in [(384 * b, 384) for b in range(7)] + [(2688, 192)]:
        third = length // 3
        row = iota((length, length), 0)
        column = iota((length, length), 1)
        order = (row == 3 * (column % third) + column // third).astype(F32).astype(BF16)
        parts.append(dot_first(columns[start : start + length, :], order).astype(BF16))
    return parts


def level(nibble):
    m = nibble & 7
    twice = m + jnp.maximum(m - 4, 0) + 2 * jnp.maximum(m - 6, 0)
    return twice.astype(F32)


def unpack(words, j, scales):
    nibble = (words >> (4 * j)) & 15
    half = jnp.exp2((scales - 1).astype(F32))
    return level(nibble) * jnp.where(nibble >= 8, -half, half)


def scale_rows(ref, q, j, width):
    r = iota((32, width), 0)
    block = (3 * r + j) // 32
    rows = [ref[3 * q + n] if len(ref.shape) == 3 else ref[pl.ds(3 * q + n, 1), :] for n in range(3)]
    return jnp.where(block == 0, rows[0], jnp.where(block == 1, rows[1], rows[2]))


def dequant_in(codes, scales, out, q, base, third):
    words = codes[pl.ds(pl.multiple_of(32 * q, 32), 32), :]
    for j in range(3):
        values = unpack(words, j, scale_rows(scales, q, j, words.shape[1]))
        out[pl.ds(pl.multiple_of(base + third * j, 32), 32), :] = values.astype(BF16)


def dequant_wide(codes, scales, out, first, last):
    def step(q, carry):
        dequant_in(codes, scales, out, q, (q // 4) * 384 + (q % 4) * 32, 128)
        return carry

    lax.fori_loop(first, min(last, 28), step, 0)
    for q in range(28, last):
        dequant_in(codes, scales, out, q, 2688 + (q - 28) * 32, 64)


def layer_kernel(
    tokens_ref, routes_ref, router_ref, drafter_ref, gain, gc, gs, uc, us, dc, ds, normed_ref, wall,
    tokv, routev, routerv, agb, snd, xr, ret, wide_codes, wide_scales, dcv, dsv, wg, wu, wd, comb, wz, hid,
    maj, mnr, sall, in_sem, code_sem, zsend, zrecv, psend, precv, loc, qsend, qrecv, qloc,
    rsend, rrecv, xsend, xrecv, wsend, wrecv, wloc,
):
    group, wide, y, z, x, c = place()
    p_me = y * 8 + x * 2 + c
    sigma = 1 - 2 * c
    y4 = 2 * group + y

    def along_y(n):
        place_y = (y4 + n) % 4
        return (place_y // 2, wide_of(place_y % 2, z, x, c))

    core = (group, wide_of(y, z, x, 1 - c))
    right = (group, wide_of(y, (z + 1) % 8, x, c))
    left = (group, wide_of(y, (z + 7) % 8, x, c))
    ahead = (group, wide_of(y, (z + 8 + sigma) % 8, x, c))
    behind = (group, wide_of(y, (z + 8 - sigma) % 8, x, c))

    loads = [
        pltpu.make_async_copy(a, b, in_sem.at[n])
        for n, (a, b) in enumerate([(tokens_ref, tokv), (routes_ref, routev), (router_ref, routerv)])
    ]
    gate_codes = pltpu.make_async_copy(gc, wide_codes, code_sem.at[0])
    gate_scales = pltpu.make_async_copy(gs, wide_scales, code_sem.at[1])
    up_codes = pltpu.make_async_copy(uc, wide_codes, code_sem.at[2])
    up_scales = pltpu.make_async_copy(us, wide_scales, code_sem.at[3])
    down_codes = pltpu.make_async_copy(dc, dcv, code_sem.at[4])
    down_scales = pltpu.make_async_copy(ds, dsv, code_sem.at[5])
    for copy in loads + [gate_codes, gate_scales, down_codes, down_scales]:
        copy.start()

    barrier = pltpu.get_barrier_semaphore()
    for neighbour in (left, right, along_y(1), along_y(3)):
        pl.semaphore_signal(barrier, inc=1, device_id=neighbour, device_id_type=MESH)

    def greet(j, carry):
        p = (p_me + j) % PLANE
        pl.semaphore_signal(barrier, inc=1, device_id=(group, plane_wide(p, z)), device_id_type=MESH)
        return carry

    lax.fori_loop(1, PLANE, greet, 0)

    def greet_other(j, carry):
        p = (1 - y) * 8 + j
        pl.semaphore_signal(barrier, inc=1, device_id=(1 - group, plane_wide(p, z)), device_id_type=MESH)
        return carry

    lax.fori_loop(0, 8, greet_other, 0)

    for copy in loads:
        copy.wait()
    columns = tokv[...]
    column = 0
    for part in spread(columns):
        width = part.shape[1]
        agb[z, 0:SLABS, :, column : column + width] = part.astype(F32).reshape(SLABS, SLOT, width).astype(BF16)
        column += width
    weight = jax.nn.sigmoid(dot_first(routerv[...], columns))
    named_expert = iota((TOK, TOK), 0)
    routes, high, low = [], [], []
    for k in range(4):
        route = routev[k : k + 1, :]
        chosen = jnp.sum(jnp.where(named_expert == route, weight, 0.0), axis=0, keepdims=True)
        top = chosen.astype(BF16).astype(F32)
        routes.append(route.astype(F32))
        high.append(top)
        low.append(chosen - top)
    line = jnp.concatenate(routes + high + low + [jnp.zeros((1, D - 12 * TOK), F32)], axis=1)
    drafter = jnp.concatenate([drafter_ref[...].astype(F32), line, jnp.zeros((1, D), F32)], axis=0)
    agb[z, SLABS] = drafter.astype(BF16)
    pl.semaphore_wait(barrier, 27)

    sends = []
    halves = (pl.ds(0, 9), pl.ds(9, 8))

    def forward(s, part, device, n):
        ref = agb.at[s, halves[part]]
        copy = remote(ref, ref, zsend.at[n, part], zrecv.at[n, part], device)
        copy.start()
        sends.append(copy)

    def arrived(s, part, n):
        ref = agb.at[s, halves[part]]
        remote(ref, ref, zsend.at[n, part], zrecv.at[n, part], right).wait_recv()

    upper = (iota((TOK, TOK), 0) < iota((TOK, TOK), 1)).astype(F32).astype(BF16)
    p_rows = iota((PLANE, 1), 0)
    experts = ((p_rows // 8) * 64 + z * 8 + p_rows % 8).astype(F32)

    def plane_send(target, s, send_sem, recv_sem):
        def send(j, carry):
            p = (p_me + j) % PLANE
            across = ((p // 8 + y) % 2) * (s % 2)
            remote(
                snd.at[s, p], target.at[s, p_me], send_sem.at[s], recv_sem.at[s],
                ((group + across) % 2, plane_wide(p, z)),
            ).start()
            return carry

        lax.fori_loop(1, PLANE, send, 0)

    def plane_copies(target, s, send_sem, recv_sem):
        return remote(snd.at[s, pl.ds(0, 15)], target.at[s, pl.ds(0, 15)], send_sem.at[s], recv_sem.at[s], core)

    def relay(s):
        meta = agb[s, SLABS, :, 0 : 12 * TOK].astype(F32)[META : META + 1, :]
        named = jnp.zeros((PLANE, TOK), F32)
        weight = jnp.zeros((PLANE, TOK), F32)
        for k in range(4):
            hit = (experts == meta[:, k * TOK : (k + 1) * TOK]).astype(F32)
            value = meta[:, (4 + k) * TOK : (5 + k) * TOK] + meta[:, (8 + k) * TOK : (9 + k) * TOK]
            named = named + hit
            weight = weight + hit * value
        rank = dot(named.astype(BF16), upper)
        slot = iota((PLANE, SLOT, TOK), 1, F32)
        pick = jnp.where(rank[:, None, :] == slot, named[:, None, :], 0.0)
        rows = dot(pick.reshape(TOK, TOK).astype(BF16), agb[s, 0:SLABS].reshape(TOK, D))
        snd[s] = rows.reshape(PLANE, SLOT, D).astype(BF16)
        pltpu.make_async_copy(snd.at[s, p_me], xr.at[s, p_me], loc.at[s]).start()
        plane_send(xr, s, psend, precv)
        weighted = (pick * weight[:, None, :]).reshape(TOK, TOK).T
        top = weighted.astype(BF16)
        comb[s, 0] = top
        comb[s, 1] = (weighted - top.astype(F32)).astype(BF16)
        wz[s] = agb[s, SLABS]

    def source(d):
        return (z + 8 + d * sigma) % 8

    order_row = iota((UNITS, UNITS), 0)
    order_column = iota((UNITS, UNITS), 1)

    def experts_on(*distances):
        inputs = []
        for d in distances:
            s = source(d)
            pltpu.make_async_copy(snd.at[s, p_me], xr.at[s, p_me], loc.at[s]).wait()
            plane_copies(xr, s, psend, precv).wait_recv()
            inputs.append(xr[s].reshape(TOK, D))
        inputs = jnp.concatenate(inputs, axis=0)
        act = (jax.nn.silu(dot(inputs, wg[...])) * dot(inputs, wu[...])).astype(BF16)
        order = (order_row == 3 * (order_column % 256) + order_column // 256).astype(F32).astype(BF16)
        act = dot(act, order).astype(BF16)
        for n, d in enumerate(distances):
            hid[pl.ds(pl.multiple_of(TOK * source(d), TOK), TOK), :] = act[n * TOK : (n + 1) * TOK]

    def dequant_down(first, last):
        def step(q, carry):
            words = dcv[pl.ds(pl.multiple_of(32 * q, 32), 32), :]
            for j in range(3):
                values = unpack(words, j, scale_rows(dsv, q, j, D))
                wd[pl.ds(pl.multiple_of(256 * j + 32 * q, 32), 32), :] = values.astype(BF16)
            return carry

        lax.fori_loop(first, last, step, 0)

    def beside(n):
        if n == 0:
            gate_codes.wait()
            gate_scales.wait()
            dequant_wide(wide_codes, wide_scales, wg, 0, 16)
        elif n == 1:
            dequant_wide(wide_codes, wide_scales, wg, 16, 30)
            up_codes.start()
            up_scales.start()
        elif n == 2:
            down_codes.wait()
            down_scales.wait()
            dequant_down(0, 4)
        elif n == 3:
            dequant_down(4, 8)
        elif n == 4:
            up_codes.wait()
            up_scales.wait()
            dequant_wide(wide_codes, wide_scales, wu, 0, 14)
        elif n == 5:
            dequant_wide(wide_codes, wide_scales, wu, 14, 30)

    for part in range(2):
        forward(z, part, right, 0)
        forward(z, part, left, 1)
    relay(z)
    beside(0)
    for k in (1, 2, 3):
        back, front = (z + 8 - k) % 8, (z + k) % 8
        far = (z + 8 - 3 * sigma) % 8
        for part in range(2):
            arrived(back, part, 2 * k - 2)
            if k < 3:
                forward(back, part, right, 2 * k)
            arrived(front, part, 2 * k - 1)
            if k < 3:
                forward(front, part, left, 2 * k + 1)
            else:
                forward(far, part, ahead, 6)
            if part == 0:
                beside(2 * k - 1)
        relay(back)
        relay(front)
        beside(2 * k)
    experts_on(0, 1)
    opposite = (z + 4) % 8
    arrived(opposite, 0, 6)
    arrived(opposite, 1, 6)
    relay(opposite)
    experts_on(-1, 2)
    experts_on(-2, 3)
    experts_on(-3)
    experts_on(4)

    def down(d):
        s = source(d)
        plane_copies(xr, s, psend, precv).wait_send()
        rows = dot(hid[pl.ds(pl.multiple_of(TOK * s, TOK), TOK), :], wd[...])
        snd[s] = rows.reshape(PLANE, SLOT, D).astype(BF16)
        pltpu.make_async_copy(snd.at[s, p_me], ret.at[s, p_me], qloc.at[s]).start()
        plane_send(ret, s, qsend, qrecv)

    def combined(d):
        s = source(d)
        pltpu.make_async_copy(snd.at[s, p_me], ret.at[s, p_me], qloc.at[s]).wait()
        plane_copies(ret, s, qsend, qrecv).wait_recv()
        rows = ret[s].reshape(TOK, D)
        return dot(comb[s, 0], rows) + dot(comb[s, 1], rows)

    half_rows = (pl.ds(0, 64), pl.ds(64, 64))

    def hop(buffer, k, half, device, n):
        copy = remote(
            buffer.at[k, half_rows[half]], buffer.at[k - 1, half_rows[half]],
            rsend.at[n, k, half], rrecv.at[n, k - 1, half], device,
        )
        copy.start()
        sends.append(copy)

    def landed(buffer, k, half, n):
        ref = buffer.at[k, half_rows[half]]
        remote(ref, ref, rsend.at[n, k, half], rrecv.at[n, k, half], ahead).wait_recv()

    def join(buffer, k, half, part, device, n):
        landed(buffer, k, half, n)
        rows = half_rows[half]
        buffer[k, rows] = (buffer[k, rows].astype(F32) + part[64 * half : 64 * half + 64]).astype(BF16)
        hop(buffer, k, half, device, n)

    down(4)
    down(3)
    down(-3)
    maj[4] = combined(4).astype(BF16)
    hop(maj, 4, 0, ahead, 0)
    hop(maj, 4, 1, ahead, 0)
    down(2)
    down(-2)
    mnr[3] = combined(-3).astype(BF16)
    hop(mnr, 3, 0, behind, 1)
    hop(mnr, 3, 1, behind, 1)
    part = combined(3)
    join(maj, 3, 0, part, ahead, 0)
    join(maj, 3, 1, part, ahead, 0)
    down(1)
    down(-1)
    part, minor = combined(2), combined(-2)
    for half in range(2):
        join(mnr, 2, half, minor, behind, 1)
        join(maj, 2, half, part, ahead, 0)
    down(0)

    keep = pltpu.make_async_copy(wz, wall.at[x], wloc)
    keep.start()

    def share_x(j, carry):
        remote(wz, wall.at[x], wsend, wrecv, (group, wide_of(y, z, (x + j) % 4, c))).start()
        return carry

    lax.fori_loop(1, 4, share_x, 0)

    part, minor = combined(1), combined(-1)
    for half in range(2):
        join(mnr, 1, half, minor, behind, 1)
        join(maj, 1, half, part, ahead, 0)
    part = combined(0)

    def pass_y(owner, half, step, n):
        ref = sall.at[owner, half_rows[half]]
        copy = remote(ref, ref, xsend.at[n, half], xrecv.at[n, half], along_y(step))
        copy.start()
        sends.append(copy)

    def got_y(owner, half, n):
        ref = sall.at[owner, half_rows[half]]
        remote(ref, ref, xsend.at[n, half], xrecv.at[n, half], core).wait_recv()

    below, above, across_y = (y4 + 3) % 4, (y4 + 1) % 4, (y4 + 2) % 4
    for half, rows in enumerate(half_rows):
        landed(mnr, 0, half, 1)
        landed(maj, 0, half, 0)
        total = part[64 * half : 64 * half + 64] + mnr[0, rows].astype(F32) + maj[0, rows].astype(F32)
        sall[y4, rows] = total.astype(BF16)
        pass_y(y4, half, 1, 0)
        pass_y(y4, half, 3, 1)
    got_y(below, 0, 0)
    pass_y(below, 0, 1, 2)
    got_y(above, 1, 1)
    pass_y(above, 1, 3, 2)
    got_y(below, 1, 0)
    got_y(above, 0, 1)
    for half, rows in enumerate(half_rows):
        got_y(across_y, half, 2)
        for q in range(2):
            feature = (sall[q, rows].astype(F32) + sall[q + 2, rows].astype(F32)).astype(BF16).astype(F32)
            mean_square = jnp.sum(feature * feature, axis=1, keepdims=True) / D
            normed_ref[q, rows] = (feature * lax.rsqrt(mean_square + 1e-05) * gain[...]).astype(BF16)
    for copy in sends:
        copy.wait_send()
    for s in range(NZ):
        plane_copies(ret, s, qsend, qrecv).wait_send()
    keep.wait()
    three = remote(wall.at[pl.ds(0, 3)], wall.at[pl.ds(0, 3)], wsend, wrecv, core)
    three.wait()


def drafter_kernel(
    grad_scale, normed, wall, error_ref, grad_ref,
    nall, first, err, eall, gsum, maj, mnr, slab, fin, fsem, nsem, esem, rsend, rrecv, psend, precv, loc,
):
    group, wide, y, z, x, c = place()
    core = (group, wide_of(y, z, x, 1 - c))
    chip = z * 4 + x
    before, after = (chip + 31) % 32, (chip + 1) % 32
    before = (group, wide_of(y, before // 4, before % 4, c))
    after = (group, wide_of(y, after // 4, after % 4, c))
    sigma = 1 - 2 * c
    ahead = (group, wide_of(y, (z + 8 + sigma) % 8, x, c))
    behind = (group, wide_of(y, (z + 8 - sigma) % 8, x, c))
    me = y * 2 + c

    def mate(j):
        n = (me + j) % 4
        return (group, wide_of(n // 2, z, x, n % 2))

    def peer(j):
        return (group, wide_of(y, z, (x + j) % 4, c))

    barrier = pltpu.get_barrier_semaphore()
    for neighbour in (ahead, behind, before, after, mate(1), mate(2), mate(3), peer(1), peer(2), peer(3)):
        pl.semaphore_signal(barrier, inc=1, device_id=neighbour, device_id_type=MESH)
    pl.semaphore_wait(barrier, 10)

    keep = pltpu.make_async_copy(normed, nall.at[c], loc.at[0])
    keep.start()
    swap = remote(normed, nall.at[c], nsem.at[0], nsem.at[1], core)
    swap.start()
    lanes = pl.ds(pl.multiple_of(group * UNITS, 128), UNITS)
    keep.wait()
    swap.wait()
    follow = remote(nall.at[0, :, pl.ds(0, 16), lanes], first, fsem.at[0], fsem.at[1], before)
    follow.start()
    predicted = lax.dot_general(
        nall[...].reshape(512, D), wall[...].reshape(256, D), (((1,), (1,)), ((), ())), preferred_element_type=F32
    )
    follow.wait()

    feature, column = iota((UNITS, 256), 0), iota((UNITS, 256), 1)
    x_of, z_of, i_of = column // 64, (column // 8) % 8, column % 8
    choose = ((feature == y * 384 + z_of * 48 + x_of * 12 + c * 6 + i_of) & (i_of < 6)).astype(F32).astype(BF16)
    row = iota((TOK, 1), 0)
    last_chip = chip == 31
    for core_of in range(2):
        for y_of in range(2):
            own = nall[core_of, y_of, :, lanes].astype(F32)
            if core_of == 0:
                following = nall[1, y_of, 0:16, lanes].astype(F32)[0:1, :]
            else:
                following = jnp.where(last_chip, first[1 - y_of].astype(F32)[0:1, :], first[y_of].astype(F32)[0:1, :])
            target = jnp.where(row == TOK - 1, following, pltpu.roll(own, TOK - 1, 0)).astype(BF16)
            start = (core_of * 2 + y_of) * TOK
            residual = predicted[start : start + TOK] - dot(target, choose)
            position = wide_of(y_of, z, x, core_of) * TOK + row
            residual = jnp.where(position < 128 * TOK - 1, residual, 0.0).astype(BF16)
            err[y_of * 2 + core_of] = residual
    keep_err = pltpu.make_async_copy(err.at[me], eall.at[me], loc.at[1])
    keep_err.start()

    def send_err(j, carry):
        n = (me + j) % 4
        remote(
            err.at[n], eall.at[me], esem.at[0], esem.at[1], (group, wide_of(n // 2, z, x, n % 2))
        ).start()
        return carry

    lax.fori_loop(1, 4, send_err, 0)

    before_order, after_order = iota((256, 192), 0), iota((256, 192), 1)
    matched = before_order == (after_order // 6 % 4) * 64 + (after_order // 24) * 8 + after_order % 6
    compact = matched.astype(F32).astype(BF16)
    factors = []
    for core_of in range(2):
        for y_of in range(2):
            factors.append(dot(err[y_of * 2 + core_of], compact).T)
    factors = jnp.concatenate(factors, axis=1).astype(BF16)
    gsum[...] = dot(factors, nall[...].reshape(512, D)) * grad_scale

    def own_part(d):
        s = (z + 8 + d * sigma) % 8
        return gsum[pl.ds(pl.multiple_of(24 * s, 8), 24), :].reshape(3, SLOT, D)

    sends = []

    def hop(buffer, k, device, n):
        copy = remote(buffer.at[k], buffer.at[k - 1], rsend.at[n, k], rrecv.at[n, k - 1], device)
        copy.start()
        sends.append(copy)

    def landed(buffer, k, n):
        remote(buffer.at[k], buffer.at[k], rsend.at[n, k], rrecv.at[n, k], ahead).wait_recv()

    maj[4] = own_part(4).astype(BF16)
    hop(maj, 4, ahead, 0)
    mnr[3] = own_part(-3).astype(BF16)
    hop(mnr, 3, behind, 1)

    keep_err.wait()
    others = remote(err.at[pl.ds(0, 3)], eall.at[pl.ds(0, 3)], esem.at[0], esem.at[1], core)
    others.wait()
    mixed, where_to = iota((1024, UNITS), 0), iota((1024, UNITS), 1)
    i_of, z_of, x_of, n_of = mixed % 8, (mixed // 8) % 8, (mixed // 64) % 4, mixed // 256
    matched = where_to == (n_of // 2) * 384 + z_of * 48 + x_of * 12 + (n_of % 2) * 6 + i_of
    restore = (matched & (i_of < 6)).astype(F32).astype(BF16)
    every = jnp.concatenate([eall[n] for n in range(4)], axis=1)
    error_ref[...] = dot(every, restore).astype(BF16)

    for k in (3, 2, 1):
        landed(maj, k, 0)
        maj[k] = (maj[k].astype(F32) + own_part(k)).astype(BF16)
        hop(maj, k, ahead, 0)
        if k < 3:
            landed(mnr, k, 1)
            mnr[k] = (mnr[k].astype(F32) + own_part(-k)).astype(BF16)
            hop(mnr, k, behind, 1)
    landed(mnr, 0, 1)
    landed(maj, 0, 0)
    total = own_part(0) + mnr[0].astype(F32) + maj[0].astype(F32)
    total = total.reshape(24, D).astype(BF16)
    q, r = iota((32, 24), 0), iota((32, 24), 1)
    expand = ((q // 8) * 6 + q % 8 == r) & (q % 8 < 6)
    slab[...] = dot(expand.astype(F32).astype(BF16), total).reshape(4, SLOT, D).astype(BF16)
    keep_fin = pltpu.make_async_copy(slab.at[x], fin.at[x], loc.at[2])
    keep_fin.start()

    def send(j, carry):
        n = (x + j) % 4
        remote(slab.at[n], fin.at[x], psend, precv, (group, wide_of(y, z, n, c))).start()
        return carry

    lax.fori_loop(1, 4, send, 0)
    keep_fin.wait()
    whole = remote(slab.at[pl.ds(0, 3)], fin.at[pl.ds(0, 3)], psend, precv, core)
    whole.wait_recv()
    grad_ref[...] = jnp.sum(fin[...].astype(F32), axis=0).astype(BF16)
    whole.wait_send()
    for copy in sends:
        copy.wait_send()


def params(number=None):
    if number is None:
        return pltpu.CompilerParams(vmem_limit_bytes=62 << 20)
    return pltpu.CompilerParams(vmem_limit_bytes=62 << 20, collective_id=number, has_side_effects=True)


VM = pl.BlockSpec(memory_space=pltpu.VMEM)
ANY = pl.BlockSpec(memory_space=pl.ANY)


def out(shape, kind=BF16):
    return jax.ShapeDtypeStruct(shape, kind)


def shards(
    tokens, routes, router, gate_codes, gate_scales, up_codes, up_scales, down_codes, down_scales, norm_gain,
    drafter_weight,
):
    dma = pltpu.SemaphoreType.DMA
    frame = (NZ, PLANE, SLOT, D)
    normed, wall = pl.pallas_call(
        layer_kernel,
        out_shape=(out((2, TOK, D)), out((4, NZ, SLOT, D))),
        in_specs=[ANY] * 3 + [VM] * 2 + [ANY] * 6,
        out_specs=(VM, ANY),
        scratch_shapes=[
            pltpu.VMEM((D, TOK), BF16),
            pltpu.VMEM((4, TOK), jnp.int32),
            pltpu.VMEM((D, TOK), BF16),
            pltpu.VMEM((NZ, BLOCKS, SLOT, D), BF16),
            pltpu.VMEM(frame, BF16),
            pltpu.VMEM(frame, BF16),
            pltpu.VMEM(frame, BF16),
            pltpu.VMEM((WORDS, UNITS), jnp.int32),
            pltpu.VMEM((90, 1, UNITS), jnp.int32),
            pltpu.VMEM((256, D), jnp.int32),
            pltpu.VMEM((24, D), jnp.int32),
            pltpu.VMEM((D, UNITS), BF16),
            pltpu.VMEM((D, UNITS), BF16),
            pltpu.VMEM((UNITS, D), BF16),
            pltpu.VMEM((NZ, 2, TOK, TOK), BF16),
            pltpu.VMEM((NZ, SLOT, D), BF16),
            pltpu.VMEM((1024, UNITS), BF16),
            pltpu.VMEM((5, TOK, D), BF16),
            pltpu.VMEM((4, TOK, D), BF16),
            pltpu.VMEM((4, TOK, D), BF16),
            dma((3,)), dma((6,)), dma((7, 2)), dma((7, 2)), dma((NZ,)), dma((NZ,)), dma((NZ,)),
            dma((NZ,)), dma((NZ,)), dma((NZ,)), dma((2, 5, 2)), dma((2, 5, 2)), dma((3, 2)), dma((3, 2)),
            dma, dma, dma,
        ],
        compiler_params=params(1),
        name="layer",
    )(
        tokens.T, routes.T, router, drafter_weight, norm_gain[None, :], gate_codes[0],
        gate_scales.transpose(1, 0, 2), up_codes[0], up_scales.transpose(1, 0, 2), down_codes[0], down_scales[0],
    )
    grad_scale = 1.0 / math.sqrt(TOK * lax.axis_size("wide"))
    error, gradient = pl.pallas_call(
        functools.partial(drafter_kernel, grad_scale),
        out_shape=(out((TOK, UNITS)), out((SLOT, D))),
        in_specs=[VM] * 2,
        out_specs=(VM, VM),
        scratch_shapes=[
            pltpu.VMEM((2, 2, TOK, D), BF16),
            pltpu.VMEM((2, 16, UNITS), BF16),
            pltpu.VMEM((4, TOK, 256), BF16),
            pltpu.VMEM((4, TOK, 256), BF16),
            pltpu.VMEM((192, D), F32),
            pltpu.VMEM((5, 3, SLOT, D), BF16),
            pltpu.VMEM((4, 3, SLOT, D), BF16),
            pltpu.VMEM((4, SLOT, D), BF16),
            pltpu.VMEM((4, SLOT, D), BF16),
            dma((2,)), dma((2,)), dma((2,)), dma((2, 5)), dma((2, 5)), dma, dma, dma((3,)),
        ],
        compiler_params=params(2),
        name="drafter",
    )(normed, wall)
    return (error, gradient[:6])


def solution(mesh):
    placed = (
        P("wide", None),
        P("wide", None),
        P(),
        P("wide", None, "group"),
        P("wide", None, "group"),
        P("wide", None, "group"),
        P("wide", None, "group"),
        P("wide", "group", None),
        P("wide", "group", None),
        P(),
        P(("group", "wide"), None),
    )
    return jax.shard_map(
        shards,
        mesh=mesh,
        in_specs=placed,
        out_specs=(P("wide", "group"), P(("group", "wide"), None)),
        check_vma=False,
    )
```

```python
import functools
import math

import jax
import jax.numpy as jnp
from jax import lax
from jax.experimental import pallas as pl
from jax.experimental.pallas import tpu as pltpu
from jax.sharding import PartitionSpec as P

MESH = pl.DeviceIdType.MESH
F32 = jnp.float32
BF16 = jnp.bfloat16

D = 2880
TOK = 128
NZ = 8
PLANE = 16
SLOT = 8
SLABS = TOK // SLOT
HALF = D // 2
ALL = 2 * PLANE
UNITS = 768
WORDS = 960


def place():
    group, wide = lax.axis_index("group"), lax.axis_index("wide")
    y, z, x, c = wide // 64, (wide // 8) % 8, (wide // 2) % 4, wide % 2
    return group, wide, y, z, x, c


def wide_of(y, z, x, c):
    return y * 64 + z * 8 + x * 2 + c


def plane_wide(p, z):
    return (p // 8) * 64 + z * 8 + p % 8


def iota(shape, dim, kind=jnp.int32):
    return lax.broadcasted_iota(jnp.int32, shape, dim).astype(kind)


def dot(a, b):
    return jnp.dot(a, b, preferred_element_type=F32)


def dot_first(a, b):
    return lax.dot_general(a, b, (((0,), (0,)), ((), ())), preferred_element_type=F32)


def remote(src, dst, send, recv, device):
    return pltpu.make_async_remote_copy(
        src_ref=src, dst_ref=dst, send_sem=send, recv_sem=recv, device_id=device, device_id_type=MESH
    )


def spread(columns):
    parts = []
    for start, length in [(0, 384), (384, 384), (768, 384), (1152, 288)]:
        third = length // 3
        row = iota((length, length), 0)
        column = iota((length, length), 1)
        order = (row == 3 * (column % third) + column // third).astype(F32).astype(BF16)
        parts.append(dot_first(columns[start : start + length, :], order).astype(BF16))
    return parts


def level(nibble):
    m = nibble & 7
    twice = m + jnp.maximum(m - 4, 0) + 2 * jnp.maximum(m - 6, 0)
    return twice.astype(F32)


def unpack(words, j, scales):
    nibble = (words >> (4 * j)) & 15
    half = jnp.exp2((scales - 1).astype(F32))
    return level(nibble) * jnp.where(nibble >= 8, -half, half)


def scale_rows(ref, q, j, width):
    r = iota((32, width), 0)
    block = (3 * r + j) // 32
    rows = [ref[3 * q + n] for n in range(3)]
    return jnp.where(block == 0, rows[0], jnp.where(block == 1, rows[1], rows[2]))


def dequant_in(codes, scales, out, q, base, third):
    words = codes[pl.ds(pl.multiple_of(32 * q, 32), 32), :]
    for j in range(3):
        values = unpack(words, j, scale_rows(scales, q, j, words.shape[1]))
        out[pl.ds(pl.multiple_of(base + third * j, 32), 32), :] = values.astype(BF16)


def dequant_wide(codes, scales, out, half):
    def step(n, carry):
        dequant_in(codes, scales, out, 15 * half + n, HALF * half + (n // 4) * 384 + (n % 4) * 32, 128)
        return carry

    lax.fori_loop(0, 12, step, 0)
    for n in range(3):
        dequant_in(codes, scales, out, 15 * half + 12 + n, HALF * half + 1152 + 32 * n, 96)


def layer_kernel(
    tokens_ref, routes_ref, router_ref, drafter_ref, gain, gc, gs, uc, us, dc, ds, normed_ref, wall,
    tokv, routev, routerv, agb, snd, xr, back_rows, ret, wide_codes, wide_scales, dcv, dsv, dsh, wg, wu, wd, comb, metas, slab, hid,
    maj, mnr, sall, in_sem, code_sem, zsend, zrecv, psend, precv, loc, qsend, qrecv, qloc,
    rsend, rrecv, xsend, xrecv, wsend, wrecv, wloc,
):
    group, wide, y, z, x, c = place()
    me = group * PLANE + y * 8 + x * 2 + c
    sigma = 1 - 2 * c
    y4 = 2 * group + y

    def along_y(n):
        place_y = (y4 + n) % 4
        return (place_y // 2, wide_of(place_y % 2, z, x, c))

    core = (group, wide_of(y, z, x, 1 - c))
    right = (group, wide_of(y, (z + 1) % 8, x, c))
    left = (group, wide_of(y, (z + 7) % 8, x, c))
    ahead = (group, wide_of(y, (z + 8 + sigma) % 8, x, c))
    behind = (group, wide_of(y, (z + 8 - sigma) % 8, x, c))

    loads = [
        pltpu.make_async_copy(a, b, in_sem.at[n])
        for n, (a, b) in enumerate([(tokens_ref, tokv), (routes_ref, routev), (router_ref, routerv)])
    ]
    gate_codes = pltpu.make_async_copy(gc, wide_codes, code_sem.at[0])
    gate_scales = pltpu.make_async_copy(gs, wide_scales, code_sem.at[1])
    up_codes = pltpu.make_async_copy(uc, wide_codes, code_sem.at[2])
    up_scales = pltpu.make_async_copy(us, wide_scales, code_sem.at[3])
    down_codes = pltpu.make_async_copy(dc, dcv, code_sem.at[4])
    down_scales = pltpu.make_async_copy(ds, dsv, code_sem.at[5])
    for copy in loads + [gate_codes, gate_scales, down_codes, down_scales]:
        copy.start()

    barrier = pltpu.get_barrier_semaphore()
    for neighbour in (left, right):
        pl.semaphore_signal(barrier, inc=1, device_id=neighbour, device_id_type=MESH)

    def plane_device(n):
        return (n // PLANE, plane_wide(n % PLANE, z))

    def greet(j, carry):
        pl.semaphore_signal(barrier, inc=1, device_id=plane_device((me + j) % ALL), device_id_type=MESH)
        return carry

    lax.fori_loop(1, ALL, greet, 0)

    for copy in loads:
        copy.wait()
    columns = tokv[...]
    column = 0
    for part in spread(tokv[pl.ds(pl.multiple_of(HALF * group, 16), HALF), :]):
        width = part.shape[1]
        agb[z, :, :, column : column + width] = part.astype(F32).reshape(SLABS, SLOT, width).astype(BF16)
        column += width
    weight = jax.nn.sigmoid(dot_first(routerv[...], columns))
    named_expert = iota((TOK, TOK), 0)
    routes, high, low = [], [], []
    for k in range(4):
        route = routev[k : k + 1, :]
        chosen = jnp.sum(jnp.where(named_expert == route, weight, 0.0), axis=0, keepdims=True)
        top = chosen.astype(BF16).astype(F32)
        routes.append(route.astype(F32))
        high.append(top)
        low.append(chosen - top)
    line = jnp.concatenate(routes + high + low, axis=1)
    metas[z] = jnp.broadcast_to(line, (SLOT, 12 * TOK)).astype(BF16)
    slab[...] = jnp.concatenate([drafter_ref[...].astype(F32), jnp.zeros((2, D), F32)], axis=0).astype(BF16)
    pl.semaphore_wait(barrier, 33)

    sends = []
    def pass_z(ref, device, n, part):
        copy = remote(ref, ref, zsend.at[n, part], zrecv.at[n, part], device)
        copy.start()
        sends.append(copy)

    def forward(s, device, n):
        pass_z(metas.at[s], device, n, 0)
        pass_z(agb.at[s], device, n, 1)

    def got_z(ref, n, part):
        remote(ref, ref, zsend.at[n, part], zrecv.at[n, part], right).wait_recv()

    def arrived(s, n):
        got_z(metas.at[s], n, 0)
        got_z(agb.at[s], n, 1)

    upper = (iota((TOK, TOK), 0) < iota((TOK, TOK), 1)).astype(F32).astype(BF16)
    p_rows = iota((PLANE, 1), 0)
    experts = ((p_rows // 8) * 64 + z * 8 + p_rows % 8).astype(F32)

    def plane_send(start, source, target, s, send_sem, recv_sem):
        def send(j, carry):
            n = (me + j) % ALL
            remote(
                source.at[s, n % start], target.at[s, me], send_sem.at[s], recv_sem.at[s], plane_device(n)
            ).start()
            return carry

        lax.fori_loop(1, ALL, send, 0)

    def plane_copies(target, s, send_sem, recv_sem):
        ref = target.at[s, pl.ds(0, ALL - 1)]
        return remote(ref, ref, send_sem.at[s], recv_sem.at[s], core)

    def relay(s):
        meta = metas[s].astype(F32)[0:1, :]
        named = jnp.zeros((PLANE, TOK), F32)
        weight = jnp.zeros((PLANE, TOK), F32)
        for k in range(4):
            hit = (experts == meta[:, k * TOK : (k + 1) * TOK]).astype(F32)
            value = meta[:, (4 + k) * TOK : (5 + k) * TOK] + meta[:, (8 + k) * TOK : (9 + k) * TOK]
            named = named + hit
            weight = weight + hit * value
        rank = dot(named.astype(BF16), upper)
        slot = iota((PLANE, SLOT, TOK), 1, F32)
        pick = jnp.where(rank[:, None, :] == slot, named[:, None, :], 0.0)
        rows = dot(pick.reshape(TOK, TOK).astype(BF16), agb[s].reshape(TOK, HALF))
        snd[s] = rows.reshape(PLANE, SLOT, HALF).astype(BF16)
        pltpu.make_async_copy(snd.at[s, me % PLANE], xr.at[s, me], loc.at[s]).start()
        plane_send(PLANE, snd, xr, s, psend, precv)
        weighted = (pick * weight[:, None, :]).reshape(TOK, TOK).T
        weighted = jnp.concatenate([weighted, weighted], axis=1)
        top = weighted.astype(BF16)
        comb[s, 0] = top
        comb[s, 1] = (weighted - top.astype(F32)).astype(BF16)

    def source(d):
        return (z + 8 + d * sigma) % 8

    order_row = iota((UNITS, UNITS), 0)
    order_column = iota((UNITS, UNITS), 1)

    def experts_on(*distances):
        lower, upper_half = [], []
        for d in distances:
            s = source(d)
            pltpu.make_async_copy(snd.at[s, 0], xr.at[s, 0], loc.at[s]).wait()
            plane_copies(xr, s, psend, precv).wait_recv()
            lower.append(xr[s, 0:PLANE].reshape(TOK, HALF))
            upper_half.append(xr[s, PLANE:ALL].reshape(TOK, HALF))
        lower = jnp.concatenate(lower, axis=0)
        upper_half = jnp.concatenate(upper_half, axis=0)
        gate = dot(lower, wg[0:HALF]) + dot(upper_half, wg[HALF:D])
        act = (jax.nn.silu(gate) * (dot(lower, wu[0:HALF]) + dot(upper_half, wu[HALF:D]))).astype(BF16)
        order = (order_row == 3 * (order_column % 256) + order_column // 256).astype(F32).astype(BF16)
        act = dot(act, order).astype(BF16)
        for n, d in enumerate(distances):
            hid[pl.ds(pl.multiple_of(TOK * source(d), TOK), TOK), :] = act[n * TOK : (n + 1) * TOK]

    def dequant_down(half):
        def block(start, width):
            columns = dcv[pl.ds(pl.multiple_of(HALF * half + start, 32), width), :].T
            lanes = pl.ds(start if width < 128 else pl.multiple_of(start, 128), width)
            for q in range(8):
                for j in range(3):
                    r = iota((32, width), 0)
                    unit = (3 * r + j) // 32
                    rows = [dsh[half, 3 * q + n : 3 * q + n + 1, lanes] for n in range(3)]
                    scales = jnp.where(unit == 0, rows[0], jnp.where(unit == 1, rows[1], rows[2]))
                    values = unpack(columns[32 * q : 32 * q + 32], j, scales)
                    wd[half, 256 * j + 32 * q : 256 * j + 32 * q + 32, lanes] = values.astype(BF16)

        def step(n, carry):
            block(128 * n, 128)
            return carry

        lax.fori_loop(0, 11, step, 0)
        block(1408, 32)

    def beside(n):
        if n == 0:
            gate_codes.wait()
            gate_scales.wait()
            dequant_wide(wide_codes, wide_scales, wg, 0)
        elif n == 1:
            dequant_wide(wide_codes, wide_scales, wg, 1)
            up_codes.start()
            up_scales.start()
        elif n == 2:
            down_codes.wait()
            down_scales.wait()
            for half in range(2):
                dsh[half] = dsv[:, HALF * half : HALF * half + HALF]
            dequant_down(0)
        elif n == 3:
            up_codes.wait()
            up_scales.wait()
            dequant_wide(wide_codes, wide_scales, wu, 0)
        elif n == 4:
            dequant_wide(wide_codes, wide_scales, wu, 1)
        elif n == 5:
            dequant_down(1)

    keep = pltpu.make_async_copy(slab, wall.at[z, x], wloc)
    keep.start()

    def share_x(j, carry):
        remote(slab, wall.at[z, x], wsend, wrecv, (group, wide_of(y, z, (x + j) % 4, c))).start()
        return carry

    lax.fori_loop(1, 4, share_x, 0)
    three = remote(wall.at[z, pl.ds(0, 3)], wall.at[z, pl.ds(0, 3)], wsend, wrecv, core)
    forward(z, right, 0)
    forward(z, left, 1)
    relay(z)
    keep.wait()
    three.wait()
    pass_z(wall.at[z], right, 0, 2)
    pass_z(wall.at[z], left, 1, 2)
    for k in (1, 2, 3):
        beside(k - 1)
        back, front = (z + 8 - k) % 8, (z + k) % 8
        arrived(back, 2 * k - 2)
        if k < 3:
            forward(back, right, 2 * k)
        arrived(front, 2 * k - 1)
        if k < 3:
            forward(front, left, 2 * k + 1)
        else:
            forward((z + 8 - 3 * sigma) % 8, ahead, 6)
        relay(back)
        relay(front)
        got_z(wall.at[back], 2 * k - 2, 2)
        if k < 3:
            pass_z(wall.at[back], right, 2 * k, 2)
        got_z(wall.at[front], 2 * k - 1, 2)
        if k < 3:
            pass_z(wall.at[front], left, 2 * k + 1, 2)
        else:
            pass_z(wall.at[(z + 8 - 3 * sigma) % 8], ahead, 6, 2)
    beside(3)
    opposite = (z + 4) % 8
    arrived(opposite, 6)
    relay(opposite)
    got_z(wall.at[opposite], 6, 2)
    beside(4)
    experts_on(0, 1)
    beside(5)
    experts_on(-1, 2)
    experts_on(-2, 3)
    experts_on(-3)

    def down(d):
        s = source(d)
        acts = hid[pl.ds(pl.multiple_of(TOK * s, TOK), TOK), :]
        for half in range(2):
            rows = dot(acts, wd[half])
            back_rows[s, PLANE * half : PLANE * half + PLANE] = rows.reshape(PLANE, SLOT, HALF).astype(BF16)
        pltpu.make_async_copy(back_rows.at[s, me], ret.at[s, me], qloc.at[s]).start()
        plane_send(ALL, back_rows, ret, s, qsend, qrecv)

    def combined(d):
        s = source(d)
        pltpu.make_async_copy(back_rows.at[s, me], ret.at[s, me], qloc.at[s]).wait()
        plane_copies(ret, s, qsend, qrecv).wait_recv()
        rows = ret[s].reshape(2 * TOK, HALF)
        return dot(comb[s, 0], rows) + dot(comb[s, 1], rows)

    def hop(buffer, k, device, n):
        copy = remote(buffer.at[k], buffer.at[k - 1], rsend.at[n, k], rrecv.at[n, k - 1], device)
        copy.start()
        sends.append(copy)

    def landed(buffer, k, n):
        remote(buffer.at[k], buffer.at[k], rsend.at[n, k], rrecv.at[n, k], ahead).wait_recv()

    def join(buffer, k, part, device, n):
        landed(buffer, k, n)
        buffer[k] = (buffer[k].astype(F32) + part).astype(BF16)
        hop(buffer, k, device, n)

    down(3)
    down(-3)
    experts_on(4)
    down(4)
    maj[4] = combined(4).astype(BF16)
    hop(maj, 4, ahead, 0)
    down(2)
    down(-2)
    part, minor = combined(3), combined(-3)
    mnr[3] = minor.astype(BF16)
    hop(mnr, 3, behind, 1)
    join(maj, 3, part, ahead, 0)
    down(1)
    down(-1)
    part, minor = combined(2), combined(-2)
    join(mnr, 2, minor, behind, 1)
    join(maj, 2, part, ahead, 0)
    down(0)

    part, minor = combined(1), combined(-1)
    join(mnr, 1, minor, behind, 1)
    join(maj, 1, part, ahead, 0)
    part = combined(0)

    half_rows = (pl.ds(0, 64), pl.ds(64, 64))

    def pass_y(owner, half, step, n):
        ref = sall.at[owner, half_rows[half]]
        copy = remote(ref, ref, xsend.at[n, half], xrecv.at[n, half], along_y(step))
        copy.start()
        sends.append(copy)

    def got_y(owner, half, n):
        ref = sall.at[owner, half_rows[half]]
        remote(ref, ref, xsend.at[n, half], xrecv.at[n, half], core).wait_recv()

    below, above, across_y = (y4 + 3) % 4, (y4 + 1) % 4, (y4 + 2) % 4
    landed(mnr, 0, 1)
    landed(maj, 0, 0)
    sall[y4] = (part + mnr[0].astype(F32) + maj[0].astype(F32)).astype(BF16)
    for half in range(2):
        pass_y(y4, half, 1, 0)
        pass_y(y4, half, 3, 1)
    got_y(below, 0, 0)
    pass_y(below, 0, 1, 2)
    got_y(above, 1, 1)
    pass_y(above, 1, 3, 2)
    got_y(below, 1, 0)
    got_y(above, 0, 1)
    for half, rows in enumerate(half_rows):
        got_y(across_y, half, 2)
        for q in range(2):
            feature = jnp.concatenate([sall[q, rows].astype(F32), sall[q + 2, rows].astype(F32)], axis=1)
            mean_square = jnp.sum(feature * feature, axis=1, keepdims=True) / D
            normed_ref[q, rows] = (feature * lax.rsqrt(mean_square + 1e-05) * gain[...].reshape(1, D)).astype(BF16)
    for copy in sends:
        copy.wait_send()
    for s in range(NZ):
        plane_copies(xr, s, psend, precv).wait_send()
        plane_copies(ret, s, qsend, qrecv).wait_send()


def drafter_kernel(
    grad_scale, normed, wall, error_ref, grad_ref,
    nall, first, err, eall, gsum, maj, mnr, slab, fin, fsem, nsem, esem, rsend, rrecv, psend, precv, loc,
):
    group, wide, y, z, x, c = place()
    core = (group, wide_of(y, z, x, 1 - c))
    chip = z * 4 + x
    before, after = (chip + 31) % 32, (chip + 1) % 32
    before = (group, wide_of(y, before // 4, before % 4, c))
    after = (group, wide_of(y, after // 4, after % 4, c))
    sigma = 1 - 2 * c
    ahead = (group, wide_of(y, (z + 8 + sigma) % 8, x, c))
    behind = (group, wide_of(y, (z + 8 - sigma) % 8, x, c))
    me = y * 2 + c

    def mate(j):
        n = (me + j) % 4
        return (group, wide_of(n // 2, z, x, n % 2))

    def peer(j):
        return (group, wide_of(y, z, (x + j) % 4, c))

    barrier = pltpu.get_barrier_semaphore()
    for neighbour in (ahead, behind, before, after, mate(1), mate(2), mate(3), peer(1), peer(2), peer(3)):
        pl.semaphore_signal(barrier, inc=1, device_id=neighbour, device_id_type=MESH)
    pl.semaphore_wait(barrier, 10)

    keep = pltpu.make_async_copy(normed, nall.at[c], loc.at[0])
    keep.start()
    swap = remote(normed, nall.at[c], nsem.at[0], nsem.at[1], core)
    swap.start()
    lanes = pl.ds(pl.multiple_of(group * UNITS, 128), UNITS)
    keep.wait()
    swap.wait()
    follow = remote(nall.at[0, :, pl.ds(0, 16), lanes], first, fsem.at[0], fsem.at[1], before)
    follow.start()
    predicted = lax.dot_general(
        nall[...].reshape(512, D), wall[...].reshape(256, D), (((1,), (1,)), ((), ())), preferred_element_type=F32
    )
    follow.wait()

    feature, column = iota((UNITS, 256), 0), iota((UNITS, 256), 1)
    x_of, z_of, i_of = (column // 8) % 4, column // 32, column % 8
    choose = ((feature == y * 384 + z_of * 48 + x_of * 12 + c * 6 + i_of) & (i_of < 6)).astype(F32).astype(BF16)
    row = iota((TOK, 1), 0)
    last_chip = chip == 31
    for core_of in range(2):
        for y_of in range(2):
            own = nall[core_of, y_of, :, lanes].astype(F32)
            if core_of == 0:
                following = nall[1, y_of, 0:16, lanes].astype(F32)[0:1, :]
            else:
                following = jnp.where(last_chip, first[1 - y_of].astype(F32)[0:1, :], first[y_of].astype(F32)[0:1, :])
            target = jnp.where(row == TOK - 1, following, pltpu.roll(own, TOK - 1, 0)).astype(BF16)
            start = (core_of * 2 + y_of) * TOK
            residual = predicted[start : start + TOK] - dot(target, choose)
            position = wide_of(y_of, z, x, core_of) * TOK + row
            residual = jnp.where(position < 128 * TOK - 1, residual, 0.0).astype(BF16)
            err[y_of * 2 + core_of] = residual
    keep_err = pltpu.make_async_copy(err.at[me], eall.at[me], loc.at[1])
    keep_err.start()

    def send_err(j, carry):
        n = (me + j) % 4
        remote(
            err.at[n], eall.at[me], esem.at[0], esem.at[1], (group, wide_of(n // 2, z, x, n % 2))
        ).start()
        return carry

    lax.fori_loop(1, 4, send_err, 0)

    before_order, after_order = iota((256, 192), 0), iota((256, 192), 1)
    matched = before_order == (after_order // 6 % 4) * 8 + (after_order // 24) * 32 + after_order % 6
    compact = matched.astype(F32).astype(BF16)
    factors = []
    for core_of in range(2):
        for y_of in range(2):
            factors.append(dot(err[y_of * 2 + core_of], compact).T)
    factors = jnp.concatenate(factors, axis=1).astype(BF16)
    gsum[...] = dot(factors, nall[...].reshape(512, D)) * grad_scale

    def own_part(d):
        s = (z + 8 + d * sigma) % 8
        return gsum[pl.ds(pl.multiple_of(24 * s, 8), 24), :].reshape(3, SLOT, D)

    sends = []

    def hop(buffer, k, device, n):
        copy = remote(buffer.at[k], buffer.at[k - 1], rsend.at[n, k], rrecv.at[n, k - 1], device)
        copy.start()
        sends.append(copy)

    def landed(buffer, k, n):
        remote(buffer.at[k], buffer.at[k], rsend.at[n, k], rrecv.at[n, k], ahead).wait_recv()

    maj[4] = own_part(4).astype(BF16)
    hop(maj, 4, ahead, 0)
    mnr[3] = own_part(-3).astype(BF16)
    hop(mnr, 3, behind, 1)

    keep_err.wait()
    others = remote(err.at[pl.ds(0, 3)], eall.at[pl.ds(0, 3)], esem.at[0], esem.at[1], core)
    others.wait()
    mixed, where_to = iota((1024, UNITS), 0), iota((1024, UNITS), 1)
    i_of, x_of, z_of, n_of = mixed % 8, (mixed // 8) % 4, (mixed // 32) % 8, mixed // 256
    matched = where_to == (n_of // 2) * 384 + z_of * 48 + x_of * 12 + (n_of % 2) * 6 + i_of
    restore = (matched & (i_of < 6)).astype(F32).astype(BF16)
    every = jnp.concatenate([eall[n] for n in range(4)], axis=1)
    error_ref[...] = dot(every, restore).astype(BF16)

    for k in (3, 2, 1):
        landed(maj, k, 0)
        maj[k] = (maj[k].astype(F32) + own_part(k)).astype(BF16)
        hop(maj, k, ahead, 0)
        if k < 3:
            landed(mnr, k, 1)
            mnr[k] = (mnr[k].astype(F32) + own_part(-k)).astype(BF16)
            hop(mnr, k, behind, 1)
    landed(mnr, 0, 1)
    landed(maj, 0, 0)
    total = own_part(0) + mnr[0].astype(F32) + maj[0].astype(F32)
    total = total.reshape(24, D).astype(BF16)
    q, r = iota((32, 24), 0), iota((32, 24), 1)
    expand = ((q // 8) * 6 + q % 8 == r) & (q % 8 < 6)
    slab[...] = dot(expand.astype(F32).astype(BF16), total).reshape(4, SLOT, D).astype(BF16)
    keep_fin = pltpu.make_async_copy(slab.at[x], fin.at[x], loc.at[2])
    keep_fin.start()

    def send(j, carry):
        n = (x + j) % 4
        remote(slab.at[n], fin.at[x], psend, precv, (group, wide_of(y, z, n, c))).start()
        return carry

    lax.fori_loop(1, 4, send, 0)
    keep_fin.wait()
    whole = remote(slab.at[pl.ds(0, 3)], fin.at[pl.ds(0, 3)], psend, precv, core)
    whole.wait_recv()
    grad_ref[...] = jnp.sum(fin[...].astype(F32), axis=0).astype(BF16)
    whole.wait_send()
    for copy in sends:
        copy.wait_send()


def params(number=None):
    if number is None:
        return pltpu.CompilerParams(vmem_limit_bytes=62 << 20)
    return pltpu.CompilerParams(vmem_limit_bytes=62 << 20, collective_id=number, has_side_effects=True)


VM = pl.BlockSpec(memory_space=pltpu.VMEM)
ANY = pl.BlockSpec(memory_space=pl.ANY)


def out(shape, kind=BF16):
    return jax.ShapeDtypeStruct(shape, kind)


def shards(
    tokens, routes, router, gate_codes, gate_scales, up_codes, up_scales, down_codes, down_scales, norm_gain,
    drafter_weight,
):
    dma = pltpu.SemaphoreType.DMA
    frame = (NZ, PLANE, SLOT, HALF)
    double = (NZ, ALL, SLOT, HALF)
    normed, wall = pl.pallas_call(
        layer_kernel,
        out_shape=(out((2, TOK, D)), out((NZ, 4, SLOT, D))),
        in_specs=[ANY] * 3 + [VM] * 2 + [ANY] * 6,
        out_specs=(VM, ANY),
        scratch_shapes=[
            pltpu.VMEM((D, TOK), BF16),
            pltpu.VMEM((4, TOK), jnp.int32),
            pltpu.VMEM((D, TOK), BF16),
            pltpu.VMEM(frame, BF16),
            pltpu.VMEM(frame, BF16),
            pltpu.VMEM(double, BF16),
            pltpu.VMEM(double, BF16),
            pltpu.VMEM(double, BF16),
            pltpu.VMEM((WORDS, UNITS), jnp.int32),
            pltpu.VMEM((90, 1, UNITS), jnp.int32),
            pltpu.VMEM((D, 256), jnp.int32),
            pltpu.VMEM((24, D), jnp.int32),
            pltpu.VMEM((2, 24, HALF), jnp.int32),
            pltpu.VMEM((D, UNITS), BF16),
            pltpu.VMEM((D, UNITS), BF16),
            pltpu.VMEM((2, UNITS, HALF), BF16),
            pltpu.VMEM((NZ, 2, TOK, 2 * TOK), BF16),
            pltpu.VMEM((NZ, SLOT, 12 * TOK), BF16),
            pltpu.VMEM((SLOT, D), BF16),
            pltpu.VMEM((1024, UNITS), BF16),
            pltpu.VMEM((5, TOK, HALF), BF16),
            pltpu.VMEM((4, TOK, HALF), BF16),
            pltpu.VMEM((4, TOK, HALF), BF16),
            dma((3,)), dma((6,)), dma((7, 3)), dma((7, 3)), dma((NZ,)), dma((NZ,)), dma((NZ,)),
            dma((NZ,)), dma((NZ,)), dma((NZ,)), dma((2, 5)), dma((2, 5)), dma((3, 2)), dma((3, 2)),
            dma, dma, dma,
        ],
        compiler_params=params(1),
        name="layer",
    )(
        tokens.T, routes.T, router, drafter_weight, norm_gain, gate_codes[0],
        gate_scales.transpose(1, 0, 2), up_codes[0], up_scales.transpose(1, 0, 2),
        down_codes[0].T, down_scales[0],
    )
    grad_scale = 1.0 / math.sqrt(TOK * lax.axis_size("wide"))
    error, gradient = pl.pallas_call(
        functools.partial(drafter_kernel, grad_scale),
        out_shape=(out((TOK, UNITS)), out((SLOT, D))),
        in_specs=[VM] * 2,
        out_specs=(VM, VM),
        scratch_shapes=[
            pltpu.VMEM((2, 2, TOK, D), BF16),
            pltpu.VMEM((2, 16, UNITS), BF16),
            pltpu.VMEM((4, TOK, 256), BF16),
            pltpu.VMEM((4, TOK, 256), BF16),
            pltpu.VMEM((192, D), F32),
            pltpu.VMEM((5, 3, SLOT, D), BF16),
            pltpu.VMEM((4, 3, SLOT, D), BF16),
            pltpu.VMEM((4, SLOT, D), BF16),
            pltpu.VMEM((4, SLOT, D), BF16),
            dma((2,)), dma((2,)), dma((2,)), dma((2, 5)), dma((2, 5)), dma, dma, dma((3,)),
        ],
        compiler_params=params(2),
        name="drafter",
    )(normed, wall)
    return (error, gradient[:6])


def solution(mesh):
    placed = (
        P("wide", None),
        P("wide", None),
        P(),
        P("wide", None, "group"),
        P("wide", None, "group"),
        P("wide", None, "group"),
        P("wide", None, "group"),
        P("wide", "group", None),
        P("wide", "group", None),
        P(),
        P(("group", "wide"), None),
    )
    return jax.shard_map(
        shards,
        mesh=mesh,
        in_specs=placed,
        out_specs=(P("wide", "group"), P(("group", "wide"), None)),
        check_vma=False,
    )
```

```python
import functools
import math

import jax
import jax.numpy as jnp
from jax import lax
from jax.experimental import pallas as pl
from jax.experimental.pallas import tpu as pltpu
from jax.sharding import PartitionSpec as P

MESH = pl.DeviceIdType.MESH
F32 = jnp.float32
BF16 = jnp.bfloat16

D = 2880
TOK = 128
NZ = 8
PLANE = 16
SLOT = 8
SLABS = TOK // SLOT
HALF = D // 2
ALL = 2 * PLANE
UNITS = 768
WORDS = 960


def place():
    group, wide = lax.axis_index("group"), lax.axis_index("wide")
    y, z, x, c = wide // 64, (wide // 8) % 8, (wide // 2) % 4, wide % 2
    return group, wide, y, z, x, c


def wide_of(y, z, x, c):
    return y * 64 + z * 8 + x * 2 + c


def plane_wide(p, z):
    return (p // 8) * 64 + z * 8 + p % 8


def iota(shape, dim, kind=jnp.int32):
    return lax.broadcasted_iota(jnp.int32, shape, dim).astype(kind)


def dot(a, b):
    return jnp.dot(a, b, preferred_element_type=F32)


def dot_first(a, b):
    return lax.dot_general(a, b, (((0,), (0,)), ((), ())), preferred_element_type=F32)


def remote(src, dst, send, recv, device):
    return pltpu.make_async_remote_copy(
        src_ref=src, dst_ref=dst, send_sem=send, recv_sem=recv, device_id=device, device_id_type=MESH
    )


def spread(columns):
    parts = []
    for start, length in [(0, 384), (384, 384), (768, 384), (1152, 288)]:
        third = length // 3
        row = iota((length, length), 0)
        column = iota((length, length), 1)
        order = (row == 3 * (column % third) + column // third).astype(F32).astype(BF16)
        parts.append(dot_first(columns[start : start + length, :], order).astype(BF16))
    return parts


def level(nibble):
    m = nibble & 7
    twice = m + jnp.maximum(m - 4, 0) + 2 * jnp.maximum(m - 6, 0)
    return twice.astype(F32)


def unpack(words, j, scales):
    nibble = (words >> (4 * j)) & 15
    half = jnp.exp2((scales - 1).astype(F32))
    return level(nibble) * jnp.where(nibble >= 8, -half, half)


def scale_rows(ref, q, j, width):
    r = iota((32, width), 0)
    block = (3 * r + j) // 32
    rows = [ref[3 * q + n] for n in range(3)]
    return jnp.where(block == 0, rows[0], jnp.where(block == 1, rows[1], rows[2]))


def dequant_in(codes, scales, out, q, base, third):
    words = codes[pl.ds(pl.multiple_of(32 * q, 32), 32), :]
    for j in range(3):
        values = unpack(words, j, scale_rows(scales, q, j, words.shape[1]))
        out[pl.ds(pl.multiple_of(base + third * j, 32), 32), :] = values.astype(BF16)


def dequant_wide(codes, scales, out, half):
    def step(n, carry):
        dequant_in(codes, scales, out, 15 * half + n, HALF * half + (n // 4) * 384 + (n % 4) * 32, 128)
        return carry

    lax.fori_loop(0, 12, step, 0)
    for n in range(3):
        dequant_in(codes, scales, out, 15 * half + 12 + n, HALF * half + 1152 + 32 * n, 96)


def layer_kernel(
    grad_scale, tokens_ref, routes_ref, router_ref, drafter_ref, gain, gc, gs, uc, us, dc, ds, error_ref, grad_ref,
    tokv, routev, routerv, agb, snd, xr, ret, wide_codes, wide_scales, dcv, dsv, dsh, wg, wu, wd, comb, metas, slab, hid,
    maj, mnr, sall, in_sem, code_sem, zsend, zrecv, psend, precv, loc, qsend, qrecv, qloc,
    rsend, rrecv, lsend, lrecv, xsend, xrecv, wsend, wrecv, wloc,
    wall, nall, first, err, eall, gsum, gmaj, gmnr, pieces, fin, fsem, nsend, nrecv, esem, gsend, grecv, fsend, frecv, dloc,
):
    group, wide, y, z, x, c = place()
    me = group * PLANE + y * 8 + x * 2 + c
    sigma = 1 - 2 * c
    y4 = 2 * group + y

    def along_y(n):
        place_y = (y4 + n) % 4
        return (place_y // 2, wide_of(place_y % 2, z, x, c))

    core = (group, wide_of(y, z, x, 1 - c))
    right = (group, wide_of(y, (z + 1) % 8, x, c))
    left = (group, wide_of(y, (z + 7) % 8, x, c))
    ahead = (group, wide_of(y, (z + 8 + sigma) % 8, x, c))
    behind = (group, wide_of(y, (z + 8 - sigma) % 8, x, c))

    loads = [
        pltpu.make_async_copy(a, b, in_sem.at[n])
        for n, (a, b) in enumerate([(tokens_ref, tokv), (routes_ref, routev), (router_ref, routerv)])
    ]
    gate_codes = pltpu.make_async_copy(gc, wide_codes, code_sem.at[0])
    gate_scales = pltpu.make_async_copy(gs, wide_scales, code_sem.at[1])
    up_codes = pltpu.make_async_copy(uc, wide_codes, code_sem.at[2])
    up_scales = pltpu.make_async_copy(us, wide_scales, code_sem.at[3])
    down_codes = pltpu.make_async_copy(dc, dcv, code_sem.at[4])
    down_scales = pltpu.make_async_copy(ds, dsv, code_sem.at[5])
    for copy in loads + [gate_codes, gate_scales, down_codes, down_scales]:
        copy.start()

    barrier = pltpu.get_barrier_semaphore()
    chip = z * 4 + x
    before, after = (chip + 31) % 32, (chip + 1) % 32
    before = (group, wide_of(y, before // 4, before % 4, c))
    after = (group, wide_of(y, after // 4, after % 4, c))
    for neighbour in (left, right, before, after):
        pl.semaphore_signal(barrier, inc=1, device_id=neighbour, device_id_type=MESH)

    def plane_device(n):
        return (n // PLANE, plane_wide(n % PLANE, z))

    def greet(j, carry):
        pl.semaphore_signal(barrier, inc=1, device_id=plane_device((me + j) % ALL), device_id_type=MESH)
        return carry

    lax.fori_loop(1, ALL, greet, 0)

    for copy in loads:
        copy.wait()
    columns = tokv[...]
    column = 0
    for part in spread(tokv[pl.ds(pl.multiple_of(HALF * group, 16), HALF), :]):
        width = part.shape[1]
        agb[z, :, :, column : column + width] = part.astype(F32).reshape(SLABS, SLOT, width).astype(BF16)
        column += width
    weight = jax.nn.sigmoid(dot_first(routerv[...], columns))
    named_expert = iota((TOK, TOK), 0)
    routes, high, low = [], [], []
    for k in range(4):
        route = routev[k : k + 1, :]
        chosen = jnp.sum(jnp.where(named_expert == route, weight, 0.0), axis=0, keepdims=True)
        top = chosen.astype(BF16).astype(F32)
        routes.append(route.astype(F32))
        high.append(top)
        low.append(chosen - top)
    line = jnp.concatenate(routes + high + low, axis=1)
    metas[z] = jnp.broadcast_to(line, (SLOT, 12 * TOK)).astype(BF16)
    slab[...] = jnp.concatenate([drafter_ref[...].astype(F32), jnp.zeros((2, D), F32)], axis=0).astype(BF16)
    pl.semaphore_wait(barrier, 35)

    sends = []
    def pass_z(ref, device, n, part):
        copy = remote(ref, ref, zsend.at[n, part], zrecv.at[n, part], device)
        copy.start()
        sends.append(copy)

    def forward(s, device, n):
        pass_z(metas.at[s], device, n, 0)
        pass_z(agb.at[s], device, n, 1)

    def got_z(ref, n, part):
        remote(ref, ref, zsend.at[n, part], zrecv.at[n, part], right).wait_recv()

    def arrived(s, n):
        got_z(metas.at[s], n, 0)
        got_z(agb.at[s], n, 1)

    upper = (iota((TOK, TOK), 0) < iota((TOK, TOK), 1)).astype(F32).astype(BF16)
    p_rows = iota((PLANE, 1), 0)
    experts = ((p_rows // 8) * 64 + z * 8 + p_rows % 8).astype(F32)

    def plane_send(start, source, target, s, send_sem, recv_sem):
        def send(j, carry):
            n = (me + j) % ALL
            remote(
                source.at[s, n % start], target.at[s, me], send_sem.at[s], recv_sem.at[s], plane_device(n)
            ).start()
            return carry

        lax.fori_loop(1, ALL, send, 0)

    def plane_copies(target, s, send_sem, recv_sem):
        ref = target.at[s, pl.ds(0, ALL - 1)]
        return remote(ref, ref, send_sem.at[s], recv_sem.at[s], core)

    def relay(s):
        meta = metas[s].astype(F32)[0:1, :]
        named = jnp.zeros((PLANE, TOK), F32)
        weight = jnp.zeros((PLANE, TOK), F32)
        for k in range(4):
            hit = (experts == meta[:, k * TOK : (k + 1) * TOK]).astype(F32)
            value = meta[:, (4 + k) * TOK : (5 + k) * TOK] + meta[:, (8 + k) * TOK : (9 + k) * TOK]
            named = named + hit
            weight = weight + hit * value
        rank = dot(named.astype(BF16), upper)
        slot = iota((PLANE, SLOT, TOK), 1, F32)
        pick = jnp.where(rank[:, None, :] == slot, named[:, None, :], 0.0)
        rows = dot(pick.reshape(TOK, TOK).astype(BF16), agb[s].reshape(TOK, HALF))
        snd[s, 0:PLANE] = rows.reshape(PLANE, SLOT, HALF).astype(BF16)
        pltpu.make_async_copy(snd.at[s, me % PLANE], xr.at[s, me], loc.at[s]).start()
        plane_send(PLANE, snd, xr, s, psend, precv)
        weighted = (pick * weight[:, None, :]).reshape(TOK, TOK).T
        weighted = jnp.concatenate([weighted, weighted], axis=1)
        top = weighted.astype(BF16)
        comb[s, 0] = top
        comb[s, 1] = (weighted - top.astype(F32)).astype(BF16)

    def source(d):
        return (z + 8 + d * sigma) % 8

    order_row = iota((UNITS, UNITS), 0)
    order_column = iota((UNITS, UNITS), 1)

    def experts_on(*distances):
        lower, upper_half = [], []
        for d in distances:
            s = source(d)
            pltpu.make_async_copy(snd.at[s, 0], xr.at[s, 0], loc.at[s]).wait()
            plane_copies(xr, s, psend, precv).wait_recv()
            lower.append(xr[s, 0:PLANE].reshape(TOK, HALF))
            upper_half.append(xr[s, PLANE:ALL].reshape(TOK, HALF))
        lower = jnp.concatenate(lower, axis=0)
        upper_half = jnp.concatenate(upper_half, axis=0)
        gate = dot(lower, wg[0:HALF]) + dot(upper_half, wg[HALF:D])
        act = (jax.nn.silu(gate) * (dot(lower, wu[0:HALF]) + dot(upper_half, wu[HALF:D]))).astype(BF16)
        order = (order_row == 3 * (order_column % 256) + order_column // 256).astype(F32).astype(BF16)
        act = dot(act, order).astype(BF16)
        for n, d in enumerate(distances):
            hid[pl.ds(pl.multiple_of(TOK * source(d), TOK), TOK), :] = act[n * TOK : (n + 1) * TOK]

    def dequant_down(half):
        def block(start, width):
            columns = dcv[pl.ds(pl.multiple_of(HALF * half + start, 32), width), :].T
            lanes = pl.ds(start if width < 128 else pl.multiple_of(start, 128), width)
            for q in range(8):
                for j in range(3):
                    r = iota((32, width), 0)
                    unit = (3 * r + j) // 32
                    rows = [dsh[half, 3 * q + n : 3 * q + n + 1, lanes] for n in range(3)]
                    scales = jnp.where(unit == 0, rows[0], jnp.where(unit == 1, rows[1], rows[2]))
                    values = unpack(columns[32 * q : 32 * q + 32], j, scales)
                    wd[half, 256 * j + 32 * q : 256 * j + 32 * q + 32, lanes] = values.astype(BF16)

        def step(n, carry):
            block(128 * n, 128)
            return carry

        lax.fori_loop(0, 11, step, 0)
        block(1408, 32)

    def beside(n):
        if n == 0:
            gate_codes.wait()
            gate_scales.wait()
            dequant_wide(wide_codes, wide_scales, wg, 0)
        elif n == 1:
            dequant_wide(wide_codes, wide_scales, wg, 1)
            up_codes.start()
            up_scales.start()
        elif n == 2:
            down_codes.wait()
            down_scales.wait()
            for half in range(2):
                dsh[half] = dsv[:, HALF * half : HALF * half + HALF]
            dequant_down(0)
        elif n == 3:
            up_codes.wait()
            up_scales.wait()
            dequant_wide(wide_codes, wide_scales, wu, 0)
        elif n == 4:
            dequant_wide(wide_codes, wide_scales, wu, 1)
        elif n == 5:
            dequant_down(1)

    keep = pltpu.make_async_copy(slab, wall.at[z, x], wloc)
    keep.start()

    def share_x(j, carry):
        remote(slab, wall.at[z, x], wsend, wrecv, (group, wide_of(y, z, (x + j) % 4, c))).start()
        return carry

    lax.fori_loop(1, 4, share_x, 0)
    three = remote(wall.at[z, pl.ds(0, 3)], wall.at[z, pl.ds(0, 3)], wsend, wrecv, core)
    forward(z, right, 0)
    forward(z, left, 1)
    relay(z)
    keep.wait()
    three.wait()
    pass_z(wall.at[z], right, 0, 2)
    pass_z(wall.at[z], left, 1, 2)
    for k in (1, 2, 3):
        beside(k - 1)
        back, front = (z + 8 - k) % 8, (z + k) % 8
        arrived(back, 2 * k - 2)
        if k < 3:
            forward(back, right, 2 * k)
        arrived(front, 2 * k - 1)
        if k < 3:
            forward(front, left, 2 * k + 1)
        else:
            forward((z + 8 - 3 * sigma) % 8, ahead, 6)
        relay(back)
        relay(front)
        got_z(wall.at[back], 2 * k - 2, 2)
        if k < 3:
            pass_z(wall.at[back], right, 2 * k, 2)
        got_z(wall.at[front], 2 * k - 1, 2)
        if k < 3:
            pass_z(wall.at[front], left, 2 * k + 1, 2)
        else:
            pass_z(wall.at[(z + 8 - 3 * sigma) % 8], ahead, 6, 2)
    beside(3)
    opposite = (z + 4) % 8
    arrived(opposite, 6)
    relay(opposite)
    got_z(wall.at[opposite], 6, 2)
    beside(4)
    experts_on(0, 1)
    beside(5)
    experts_on(-1, 2)
    experts_on(-2, 3)
    experts_on(-3)

    def down(d):
        s = source(d)
        plane_copies(xr, s, psend, precv).wait_send()
        acts = hid[pl.ds(pl.multiple_of(TOK * s, TOK), TOK), :]
        for half in range(2):
            rows = dot(acts, wd[half])
            snd[s, PLANE * half : PLANE * half + PLANE] = rows.reshape(PLANE, SLOT, HALF).astype(BF16)
        pltpu.make_async_copy(snd.at[s, me], ret.at[s, me], qloc.at[s]).start()
        plane_send(ALL, snd, ret, s, qsend, qrecv)

    def combined(d):
        s = source(d)
        pltpu.make_async_copy(snd.at[s, me], ret.at[s, me], qloc.at[s]).wait()
        plane_copies(ret, s, qsend, qrecv).wait_recv()
        rows = ret[s].reshape(2 * TOK, HALF)
        return dot(comb[s, 0], rows) + dot(comb[s, 1], rows)

    def hop(buffer, k, device, n):
        copy = remote(buffer.at[k], buffer.at[k - 1], rsend.at[n, k], rrecv.at[n, k - 1], device)
        copy.start()
        sends.append(copy)

    def landed(buffer, k, n):
        remote(buffer.at[k], buffer.at[k], rsend.at[n, k], rrecv.at[n, k], ahead).wait_recv()

    def join(buffer, k, part, device, n):
        landed(buffer, k, n)
        buffer[k] = (buffer[k].astype(F32) + part).astype(BF16)
        hop(buffer, k, device, n)

    down(3)
    down(-3)
    experts_on(4)
    down(4)
    maj[4] = combined(4).astype(BF16)
    hop(maj, 4, ahead, 0)
    down(2)
    down(-2)
    part, minor = combined(3), combined(-3)
    mnr[3] = minor.astype(BF16)
    hop(mnr, 3, behind, 1)
    join(maj, 3, part, ahead, 0)
    down(1)
    down(-1)
    part, minor = combined(2), combined(-2)
    join(mnr, 2, minor, behind, 1)
    join(maj, 2, part, ahead, 0)
    down(0)

    part, minor = combined(1), combined(-1)
    half_rows = (pl.ds(0, 64), pl.ds(64, 64))

    def last(buffer, half, device, n):
        copy = remote(
            buffer.at[1, half_rows[half]], buffer.at[0, half_rows[half]], lsend.at[n, half], lrecv.at[n, half], device
        )
        copy.start()
        sends.append(copy)

    landed(mnr, 1, 1)
    landed(maj, 1, 0)
    for half, rows in enumerate(half_rows):
        for n, (buffer, more, device) in enumerate(((maj, part, ahead), (mnr, minor, behind))):
            buffer[1, rows] = (buffer[1, rows].astype(F32) + more[64 * half : 64 * half + 64]).astype(BF16)
            last(buffer, half, device, n)
    part = combined(0)

    def pass_y(owner, half, step, n):
        ref = sall.at[owner, half_rows[half]]
        copy = remote(ref, ref, xsend.at[n, half], xrecv.at[n, half], along_y(step))
        copy.start()
        sends.append(copy)

    def got_y(owner, half, n):
        ref = sall.at[owner, half_rows[half]]
        remote(ref, ref, xsend.at[n, half], xrecv.at[n, half], core).wait_recv()

    below, above, across_y = (y4 + 3) % 4, (y4 + 1) % 4, (y4 + 2) % 4
    for half, rows in enumerate(half_rows):
        total = part[64 * half : 64 * half + 64]
        for n, buffer in enumerate((maj, mnr)):
            ref = buffer.at[0, rows]
            remote(ref, ref, lsend.at[n, half], lrecv.at[n, half], ahead).wait_recv()
            total = total + buffer[0, rows].astype(F32)
        sall[y4, rows] = total.astype(BF16)
        pass_y(y4, half, 1, 0)
        pass_y(y4, half, 3, 1)
    got_y(below, 0, 0)
    pass_y(below, 0, 1, 2)
    got_y(above, 1, 1)
    pass_y(above, 1, 3, 2)
    got_y(below, 1, 0)
    got_y(above, 0, 1)
    swaps = []
    for half, rows in enumerate(half_rows):
        got_y(across_y, half, 2)
        for q in range(2):
            feature = jnp.concatenate([sall[q, rows].astype(F32), sall[q + 2, rows].astype(F32)], axis=1)
            mean_square = jnp.sum(feature * feature, axis=1, keepdims=True) / D
            nall[c, q, rows] = (feature * lax.rsqrt(mean_square + 1e-05) * gain[...].reshape(1, D)).astype(BF16)
        ref = nall.at[c, :, rows]
        swap = remote(ref, ref, nsend.at[half], nrecv.at[half], core)
        swap.start()
        swaps.append(swap)
    lanes = pl.ds(pl.multiple_of(group * UNITS, 128), UNITS)
    for swap in swaps:
        swap.wait()
    follow = remote(nall.at[0, :, pl.ds(0, 16), lanes], first, fsem.at[0], fsem.at[1], before)
    follow.start()
    predicted = lax.dot_general(
        nall[...].reshape(512, D), wall[...].reshape(256, D), (((1,), (1,)), ((), ())), preferred_element_type=F32
    )
    follow.wait()

    feature, column = iota((UNITS, 256), 0), iota((UNITS, 256), 1)
    x_of, z_of, i_of = (column // 8) % 4, column // 32, column % 8
    choose = ((feature == y * 384 + z_of * 48 + x_of * 12 + c * 6 + i_of) & (i_of < 6)).astype(F32).astype(BF16)
    row = iota((TOK, 1), 0)
    last_chip = chip == 31
    quad = y * 2 + c
    for core_of in range(2):
        for y_of in range(2):
            own = nall[core_of, y_of, :, lanes].astype(F32)
            if core_of == 0:
                following = nall[1, y_of, 0:16, lanes].astype(F32)[0:1, :]
            else:
                following = jnp.where(last_chip, first[1 - y_of].astype(F32)[0:1, :], first[y_of].astype(F32)[0:1, :])
            target = jnp.where(row == TOK - 1, following, pltpu.roll(own, TOK - 1, 0)).astype(BF16)
            start = (core_of * 2 + y_of) * TOK
            residual = predicted[start : start + TOK] - dot(target, choose)
            position = wide_of(y_of, z, x, core_of) * TOK + row
            residual = jnp.where(position < 128 * TOK - 1, residual, 0.0).astype(BF16)
            err[y_of * 2 + core_of] = residual
    keep_err = pltpu.make_async_copy(err.at[quad], eall.at[quad], dloc.at[0])
    keep_err.start()

    def send_err(j, carry):
        n = (quad + j) % 4
        remote(
            err.at[n], eall.at[quad], esem.at[0], esem.at[1], (group, wide_of(n // 2, z, x, n % 2))
        ).start()
        return carry

    lax.fori_loop(1, 4, send_err, 0)

    before_order, after_order = iota((256, 192), 0), iota((256, 192), 1)
    matched = before_order == (after_order // 6 % 4) * 8 + (after_order // 24) * 32 + after_order % 6
    compact = matched.astype(F32).astype(BF16)
    factors = []
    for core_of in range(2):
        for y_of in range(2):
            factors.append(dot(err[y_of * 2 + core_of], compact).T)
    factors = jnp.concatenate(factors, axis=1).astype(BF16)
    gsum[...] = dot(factors, nall[...].reshape(512, D)) * grad_scale

    def own_part(d):
        s = (z + 8 + d * sigma) % 8
        return gsum[pl.ds(pl.multiple_of(24 * s, 8), 24), :].reshape(3, SLOT, D)

    def ghop(buffer, k, device, n):
        copy = remote(buffer.at[k], buffer.at[k - 1], gsend.at[n, k], grecv.at[n, k - 1], device)
        copy.start()
        sends.append(copy)

    def glanded(buffer, k, n):
        remote(buffer.at[k], buffer.at[k], gsend.at[n, k], grecv.at[n, k], ahead).wait_recv()

    gmaj[4] = own_part(4).astype(BF16)
    ghop(gmaj, 4, ahead, 0)
    gmnr[3] = own_part(-3).astype(BF16)
    ghop(gmnr, 3, behind, 1)

    keep_err.wait()
    others = remote(err.at[pl.ds(0, 3)], eall.at[pl.ds(0, 3)], esem.at[0], esem.at[1], core)
    others.wait()
    mixed, where_to = iota((1024, UNITS), 0), iota((1024, UNITS), 1)
    i_of, x_of, z_of, n_of = mixed % 8, (mixed // 8) % 4, (mixed // 32) % 8, mixed // 256
    matched = where_to == (n_of // 2) * 384 + z_of * 48 + x_of * 12 + (n_of % 2) * 6 + i_of
    restore = (matched & (i_of < 6)).astype(F32).astype(BF16)
    every = jnp.concatenate([eall[n] for n in range(4)], axis=1)
    error_ref[...] = dot(every, restore).astype(BF16)

    for k in (3, 2, 1):
        glanded(gmaj, k, 0)
        gmaj[k] = (gmaj[k].astype(F32) + own_part(k)).astype(BF16)
        ghop(gmaj, k, ahead, 0)
        if k < 3:
            glanded(gmnr, k, 1)
            gmnr[k] = (gmnr[k].astype(F32) + own_part(-k)).astype(BF16)
            ghop(gmnr, k, behind, 1)
    glanded(gmnr, 0, 1)
    glanded(gmaj, 0, 0)
    total = own_part(0) + gmnr[0].astype(F32) + gmaj[0].astype(F32)
    total = total.reshape(24, D).astype(BF16)
    q, r = iota((32, 24), 0), iota((32, 24), 1)
    expand = ((q // 8) * 6 + q % 8 == r) & (q % 8 < 6)
    pieces[...] = dot(expand.astype(F32).astype(BF16), total).reshape(4, SLOT, D).astype(BF16)
    keep_fin = pltpu.make_async_copy(pieces.at[x], fin.at[x], dloc.at[1])
    keep_fin.start()

    def send(j, carry):
        n = (x + j) % 4
        remote(pieces.at[n], fin.at[x], fsend, frecv, (group, wide_of(y, z, n, c))).start()
        return carry

    lax.fori_loop(1, 4, send, 0)
    keep_fin.wait()
    whole = remote(pieces.at[pl.ds(0, 3)], fin.at[pl.ds(0, 3)], fsend, frecv, core)
    whole.wait_recv()
    grad_ref[...] = jnp.sum(fin[...].astype(F32), axis=0).astype(BF16)
    whole.wait_send()
    for copy in sends:
        copy.wait_send()
    for s in range(NZ):
        plane_copies(ret, s, qsend, qrecv).wait_send()


def params(number=None):
    if number is None:
        return pltpu.CompilerParams(vmem_limit_bytes=62 << 20)
    return pltpu.CompilerParams(vmem_limit_bytes=62 << 20, collective_id=number, has_side_effects=True)


VM = pl.BlockSpec(memory_space=pltpu.VMEM)
ANY = pl.BlockSpec(memory_space=pl.ANY)


def out(shape, kind=BF16):
    return jax.ShapeDtypeStruct(shape, kind)


def shards(
    tokens, routes, router, gate_codes, gate_scales, up_codes, up_scales, down_codes, down_scales, norm_gain,
    drafter_weight,
):
    dma = pltpu.SemaphoreType.DMA
    frame = (NZ, PLANE, SLOT, HALF)
    double = (NZ, ALL, SLOT, HALF)
    grad_scale = 1.0 / math.sqrt(TOK * lax.axis_size("wide"))
    error, gradient = pl.pallas_call(
        functools.partial(layer_kernel, grad_scale),
        out_shape=(out((TOK, UNITS)), out((SLOT, D))),
        in_specs=[ANY] * 3 + [VM] * 2 + [ANY] * 6,
        out_specs=(VM, VM),
        scratch_shapes=[
            pltpu.VMEM((D, TOK), BF16),
            pltpu.VMEM((4, TOK), jnp.int32),
            pltpu.VMEM((D, TOK), BF16),
            pltpu.VMEM(frame, BF16),
            pltpu.VMEM(double, BF16),
            pltpu.VMEM(double, BF16),
            pltpu.VMEM(double, BF16),
            pltpu.VMEM((WORDS, UNITS), jnp.int32),
            pltpu.VMEM((90, 1, UNITS), jnp.int32),
            pltpu.VMEM((D, 256), jnp.int32),
            pltpu.VMEM((24, D), jnp.int32),
            pltpu.VMEM((2, 24, HALF), jnp.int32),
            pltpu.VMEM((D, UNITS), BF16),
            pltpu.VMEM((D, UNITS), BF16),
            pltpu.VMEM((2, UNITS, HALF), BF16),
            pltpu.VMEM((NZ, 2, TOK, 2 * TOK), BF16),
            pltpu.VMEM((NZ, SLOT, 12 * TOK), BF16),
            pltpu.VMEM((SLOT, D), BF16),
            pltpu.VMEM((1024, UNITS), BF16),
            pltpu.VMEM((5, TOK, HALF), BF16),
            pltpu.VMEM((4, TOK, HALF), BF16),
            pltpu.VMEM((4, TOK, HALF), BF16),
            dma((3,)), dma((6,)), dma((7, 3)), dma((7, 3)), dma((NZ,)), dma((NZ,)), dma((NZ,)),
            dma((NZ,)), dma((NZ,)), dma((NZ,)), dma((2, 5)), dma((2, 5)), dma((2, 2)), dma((2, 2)), dma((3, 2)), dma((3, 2)),
            dma, dma, dma,
            pltpu.VMEM((NZ, 4, SLOT, D), BF16),
            pltpu.VMEM((2, 2, TOK, D), BF16),
            pltpu.VMEM((2, 16, UNITS), BF16),
            pltpu.VMEM((4, TOK, 256), BF16),
            pltpu.VMEM((4, TOK, 256), BF16),
            pltpu.VMEM((192, D), F32),
            pltpu.VMEM((5, 3, SLOT, D), BF16),
            pltpu.VMEM((4, 3, SLOT, D), BF16),
            pltpu.VMEM((4, SLOT, D), BF16),
            pltpu.VMEM((4, SLOT, D), BF16),
            dma((2,)), dma((2,)), dma((2,)), dma((2,)), dma((2, 5)), dma((2, 5)), dma, dma, dma((2,)),
        ],
        compiler_params=params(1),
        name="layer",
    )(
        tokens.T, routes.T, router, drafter_weight, norm_gain, gate_codes[0],
        gate_scales.transpose(1, 0, 2), up_codes[0], up_scales.transpose(1, 0, 2),
        down_codes[0].T, down_scales[0],
    )
    return (error, gradient[:6])


def solution(mesh):
    placed = (
        P("wide", None),
        P("wide", None),
        P(),
        P("wide", None, "group"),
        P("wide", None, "group"),
        P("wide", None, "group"),
        P("wide", None, "group"),
        P("wide", "group", None),
        P("wide", "group", None),
        P(),
        P(("group", "wide"), None),
    )
    return jax.shard_map(
        shards,
        mesh=mesh,
        in_specs=placed,
        out_specs=(P("wide", "group"), P(("group", "wide"), None)),
        check_vma=False,
    )
```

```python
import functools
import math

import jax
import jax.numpy as jnp
from jax import lax
from jax.experimental import pallas as pl
from jax.experimental.pallas import tpu as pltpu
from jax.sharding import PartitionSpec as P

MESH = pl.DeviceIdType.MESH
F32 = jnp.float32
BF16 = jnp.bfloat16

D = 2880
TOK = 128
NZ = 8
PLANE = 16
SLOT = 8
SLABS = TOK // SLOT
HALF = D // 2
ALL = 2 * PLANE
UNITS = 768
WORDS = 960


def place():
    group, wide = lax.axis_index("group"), lax.axis_index("wide")
    y, z, x, c = wide // 64, (wide // 8) % 8, (wide // 2) % 4, wide % 2
    return group, wide, y, z, x, c


def wide_of(y, z, x, c):
    return y * 64 + z * 8 + x * 2 + c


def plane_wide(p, z):
    return (p // 8) * 64 + z * 8 + p % 8


def iota(shape, dim, kind=jnp.int32):
    return lax.broadcasted_iota(jnp.int32, shape, dim).astype(kind)


def dot(a, b):
    return jnp.dot(a, b, preferred_element_type=F32)


def dot_first(a, b):
    return lax.dot_general(a, b, (((0,), (0,)), ((), ())), preferred_element_type=F32)


def remote(src, dst, send, recv, device):
    return pltpu.make_async_remote_copy(
        src_ref=src, dst_ref=dst, send_sem=send, recv_sem=recv, device_id=device, device_id_type=MESH
    )


def spread(columns):
    parts = []
    for start, length in [(0, 384), (384, 384), (768, 384), (1152, 288)]:
        third = length // 3
        row = iota((length, length), 0)
        column = iota((length, length), 1)
        order = (row == 3 * (column % third) + column // third).astype(F32).astype(BF16)
        parts.append(dot_first(columns[start : start + length, :], order).astype(BF16))
    return parts


def level(nibble):
    m = nibble & 7
    twice = m + jnp.maximum(m - 4, 0) + 2 * jnp.maximum(m - 6, 0)
    return twice.astype(F32)


def unpack(words, j, scales):
    nibble = (words >> (4 * j)) & 15
    half = jnp.exp2((scales - 1).astype(F32))
    return level(nibble) * jnp.where(nibble >= 8, -half, half)


def scale_rows(ref, q, j, width):
    r = iota((32, width), 0)
    block = (3 * r + j) // 32
    rows = [ref[3 * q + n] for n in range(3)]
    return jnp.where(block == 0, rows[0], jnp.where(block == 1, rows[1], rows[2]))


def dequant_in(codes, scales, out, q, base, third):
    words = codes[pl.ds(pl.multiple_of(32 * q, 32), 32), :]
    for j in range(3):
        values = unpack(words, j, scale_rows(scales, q, j, words.shape[1]))
        out[pl.ds(pl.multiple_of(base + third * j, 32), 32), :] = values.astype(BF16)


def dequant_wide(codes, scales, out, half):
    def step(n, carry):
        dequant_in(codes, scales, out, 15 * half + n, HALF * half + (n // 4) * 384 + (n % 4) * 32, 128)
        return carry

    lax.fori_loop(0, 12, step, 0)
    for n in range(3):
        dequant_in(codes, scales, out, 15 * half + 12 + n, HALF * half + 1152 + 32 * n, 96)


def layer_kernel(
    grad_scale, tokens_ref, routes_ref, router_ref, drafter_ref, gain, gc, gs, uc, us, dc, ds, error_ref, grad_ref,
    tokv, routev, routerv, agb, snd, xr, ret, wide_codes, wide_scales, dcv, dsv, dsh, wg, wu, wd, comb, metas, slab, hid,
    maj, mnr, sall, in_sem, code_sem, zsend, zrecv, psend, precv, loc, qsend, qrecv, qloc,
    rsend, rrecv, lsend, lrecv, xsend, xrecv, wsend, wrecv, wloc,
    wall, nall, first, err, eall, gsum, gmaj, gmnr, pieces, fin, fsem, nsend, nrecv, esem, gsend, grecv, fsend, frecv, dloc,
):
    group, wide, y, z, x, c = place()
    me = group * PLANE + y * 8 + x * 2 + c
    sigma = 1 - 2 * c
    y4 = 2 * group + y

    def along_y(n):
        place_y = (y4 + n) % 4
        return (place_y // 2, wide_of(place_y % 2, z, x, c))

    core = (group, wide_of(y, z, x, 1 - c))
    right = (group, wide_of(y, (z + 1) % 8, x, c))
    left = (group, wide_of(y, (z + 7) % 8, x, c))
    ahead = (group, wide_of(y, (z + 8 + sigma) % 8, x, c))
    behind = (group, wide_of(y, (z + 8 - sigma) % 8, x, c))

    loads = [
        pltpu.make_async_copy(a, b, in_sem.at[n])
        for n, (a, b) in enumerate([(tokens_ref, tokv), (routes_ref, routev), (router_ref, routerv)])
    ]
    gate_codes = pltpu.make_async_copy(gc, wide_codes, code_sem.at[0])
    gate_scales = pltpu.make_async_copy(gs, wide_scales, code_sem.at[1])
    up_codes = pltpu.make_async_copy(uc, wide_codes, code_sem.at[2])
    up_scales = pltpu.make_async_copy(us, wide_scales, code_sem.at[3])
    down_codes = pltpu.make_async_copy(dc, dcv, code_sem.at[4])
    down_scales = pltpu.make_async_copy(ds, dsv, code_sem.at[5])
    for copy in loads + [gate_codes, gate_scales, down_codes, down_scales]:
        copy.start()

    barrier = pltpu.get_barrier_semaphore()
    chip = z * 4 + x
    before, after = (chip + 31) % 32, (chip + 1) % 32
    before = (group, wide_of(y, before // 4, before % 4, c))
    after = (group, wide_of(y, after // 4, after % 4, c))
    for neighbour in (left, right, before, after):
        pl.semaphore_signal(barrier, inc=1, device_id=neighbour, device_id_type=MESH)

    def plane_device(n):
        return (n // PLANE, plane_wide(n % PLANE, z))

    def greet(j, carry):
        pl.semaphore_signal(barrier, inc=1, device_id=plane_device((me + j) % ALL), device_id_type=MESH)
        return carry

    lax.fori_loop(1, ALL, greet, 0)

    for copy in loads:
        copy.wait()
    columns = tokv[...]
    column = 0
    for part in spread(tokv[pl.ds(pl.multiple_of(HALF * group, 16), HALF), :]):
        width = part.shape[1]
        agb[z, :, :, column : column + width] = part.astype(F32).reshape(SLABS, SLOT, width).astype(BF16)
        column += width
    weight = jax.nn.sigmoid(dot_first(routerv[...], columns))
    named_expert = iota((TOK, TOK), 0)
    routes, high, low = [], [], []
    for k in range(4):
        route = routev[k : k + 1, :]
        chosen = jnp.sum(jnp.where(named_expert == route, weight, 0.0), axis=0, keepdims=True)
        top = chosen.astype(BF16).astype(F32)
        routes.append(route.astype(F32))
        high.append(top)
        low.append(chosen - top)
    line = jnp.concatenate(routes + high + low, axis=1)
    metas[z] = jnp.broadcast_to(line, (SLOT, 12 * TOK)).astype(BF16)
    slab[...] = jnp.concatenate([drafter_ref[...].astype(F32), jnp.zeros((2, D), F32)], axis=0).astype(BF16)
    pl.semaphore_wait(barrier, 35)

    sends = []
    def pass_z(ref, device, n, part):
        copy = remote(ref, ref, zsend.at[n, part], zrecv.at[n, part], device)
        copy.start()
        sends.append(copy)

    def forward(s, device, n):
        pass_z(metas.at[s], device, n, 0)
        pass_z(agb.at[s], device, n, 1)

    def got_z(ref, n, part):
        remote(ref, ref, zsend.at[n, part], zrecv.at[n, part], right).wait_recv()

    def arrived(s, n):
        got_z(metas.at[s], n, 0)
        got_z(agb.at[s], n, 1)

    upper = (iota((TOK, TOK), 0) < iota((TOK, TOK), 1)).astype(F32).astype(BF16)
    p_rows = iota((PLANE, 1), 0)
    experts = ((p_rows // 8) * 64 + z * 8 + p_rows % 8).astype(F32)

    def plane_send(start, source, target, s, send_sem, recv_sem):
        def send(j, carry):
            n = (me + j) % ALL
            remote(
                source.at[s, n % start], target.at[s, me], send_sem.at[s], recv_sem.at[s], plane_device(n)
            ).start()
            return carry

        lax.fori_loop(1, ALL, send, 0)

    def plane_copies(target, s, send_sem, recv_sem):
        ref = target.at[s, pl.ds(0, ALL - 1)]
        return remote(ref, ref, send_sem.at[s], recv_sem.at[s], core)

    def relay(s):
        meta = metas[s].astype(F32)[0:1, :]
        named = jnp.zeros((PLANE, TOK), F32)
        weight = jnp.zeros((PLANE, TOK), F32)
        for k in range(4):
            hit = (experts == meta[:, k * TOK : (k + 1) * TOK]).astype(F32)
            value = meta[:, (4 + k) * TOK : (5 + k) * TOK] + meta[:, (8 + k) * TOK : (9 + k) * TOK]
            named = named + hit
            weight = weight + hit * value
        rank = dot(named.astype(BF16), upper)
        slot = iota((PLANE, SLOT, TOK), 1, F32)
        pick = jnp.where(rank[:, None, :] == slot, named[:, None, :], 0.0)
        rows = dot(pick.reshape(TOK, TOK).astype(BF16), agb[s].reshape(TOK, HALF))
        snd[s, 0:PLANE] = rows.reshape(PLANE, SLOT, HALF).astype(BF16)
        pltpu.make_async_copy(snd.at[s, me % PLANE], xr.at[s, me], loc.at[s]).start()
        plane_send(PLANE, snd, xr, s, psend, precv)
        weighted = (pick * weight[:, None, :]).reshape(TOK, TOK).T
        weighted = jnp.concatenate([weighted, weighted], axis=1)
        top = weighted.astype(BF16)
        comb[s, 0] = top
        comb[s, 1] = (weighted - top.astype(F32)).astype(BF16)

    def source(d):
        return (z + 8 + d * sigma) % 8

    order_row = iota((UNITS, UNITS), 0)
    order_column = iota((UNITS, UNITS), 1)

    def experts_on(*distances):
        lower, upper_half = [], []
        for d in distances:
            s = source(d)
            pltpu.make_async_copy(snd.at[s, 0], xr.at[s, 0], loc.at[s]).wait()
            plane_copies(xr, s, psend, precv).wait_recv()
            lower.append(xr[s, 0:PLANE].reshape(TOK, HALF))
            upper_half.append(xr[s, PLANE:ALL].reshape(TOK, HALF))
        lower = jnp.concatenate(lower, axis=0)
        upper_half = jnp.concatenate(upper_half, axis=0)
        gate = dot(lower, wg[0:HALF]) + dot(upper_half, wg[HALF:D])
        act = (jax.nn.silu(gate) * (dot(lower, wu[0:HALF]) + dot(upper_half, wu[HALF:D]))).astype(BF16)
        order = (order_row == 3 * (order_column % 256) + order_column // 256).astype(F32).astype(BF16)
        act = dot(act, order).astype(BF16)
        for n, d in enumerate(distances):
            hid[pl.ds(pl.multiple_of(TOK * source(d), TOK), TOK), :] = act[n * TOK : (n + 1) * TOK]

    def dequant_down(half):
        def block(start, width):
            columns = dcv[pl.ds(pl.multiple_of(HALF * half + start, 32), width), :].T
            lanes = pl.ds(start if width < 128 else pl.multiple_of(start, 128), width)
            for q in range(8):
                for j in range(3):
                    r = iota((32, width), 0)
                    unit = (3 * r + j) // 32
                    rows = [dsh[half, 3 * q + n : 3 * q + n + 1, lanes] for n in range(3)]
                    scales = jnp.where(unit == 0, rows[0], jnp.where(unit == 1, rows[1], rows[2]))
                    values = unpack(columns[32 * q : 32 * q + 32], j, scales)
                    wd[half, 256 * j + 32 * q : 256 * j + 32 * q + 32, lanes] = values.astype(BF16)

        def step(n, carry):
            block(128 * n, 128)
            return carry

        lax.fori_loop(0, 11, step, 0)
        block(1408, 32)

    def beside(n):
        if n == 0:
            gate_codes.wait()
            gate_scales.wait()
            dequant_wide(wide_codes, wide_scales, wg, 0)
        elif n == 1:
            dequant_wide(wide_codes, wide_scales, wg, 1)
            up_codes.start()
            up_scales.start()
        elif n == 2:
            down_codes.wait()
            down_scales.wait()
            for half in range(2):
                dsh[half] = dsv[:, HALF * half : HALF * half + HALF]
            dequant_down(0)
        elif n == 3:
            up_codes.wait()
            up_scales.wait()
            dequant_wide(wide_codes, wide_scales, wu, 0)
        elif n == 4:
            dequant_wide(wide_codes, wide_scales, wu, 1)
        elif n == 5:
            dequant_down(1)

    keep = pltpu.make_async_copy(slab, wall.at[z, x], wloc)
    keep.start()

    def share_x(j, carry):
        remote(slab, wall.at[z, x], wsend, wrecv, (group, wide_of(y, z, (x + j) % 4, c))).start()
        return carry

    lax.fori_loop(1, 4, share_x, 0)
    three = remote(wall.at[z, pl.ds(0, 3)], wall.at[z, pl.ds(0, 3)], wsend, wrecv, core)
    forward(z, right, 0)
    forward(z, left, 1)
    relay(z)
    keep.wait()
    three.wait()
    pass_z(wall.at[z], right, 0, 2)
    pass_z(wall.at[z], left, 1, 2)
    for k in (1, 2, 3):
        beside(k - 1)
        back, front = (z + 8 - k) % 8, (z + k) % 8
        arrived(back, 2 * k - 2)
        if k < 3:
            forward(back, right, 2 * k)
        arrived(front, 2 * k - 1)
        if k < 3:
            forward(front, left, 2 * k + 1)
        else:
            forward((z + 8 - 3 * sigma) % 8, ahead, 6)
        relay(back)
        relay(front)
        got_z(wall.at[back], 2 * k - 2, 2)
        if k < 3:
            pass_z(wall.at[back], right, 2 * k, 2)
        got_z(wall.at[front], 2 * k - 1, 2)
        if k < 3:
            pass_z(wall.at[front], left, 2 * k + 1, 2)
        else:
            pass_z(wall.at[(z + 8 - 3 * sigma) % 8], ahead, 6, 2)
    beside(3)
    opposite = (z + 4) % 8
    arrived(opposite, 6)
    relay(opposite)
    got_z(wall.at[opposite], 6, 2)
    beside(4)
    experts_on(0, 1)
    beside(5)
    experts_on(-1, 2)
    experts_on(-2, 3)
    experts_on(-3)

    def down(d):
        s = source(d)
        plane_copies(xr, s, psend, precv).wait_send()
        acts = hid[pl.ds(pl.multiple_of(TOK * s, TOK), TOK), :]
        for half in range(2):
            rows = dot(acts, wd[half])
            snd[s, PLANE * half : PLANE * half + PLANE] = rows.reshape(PLANE, SLOT, HALF).astype(BF16)
        pltpu.make_async_copy(snd.at[s, me], ret.at[s, me], qloc.at[s]).start()
        plane_send(ALL, snd, ret, s, qsend, qrecv)

    def combined(d):
        s = source(d)
        pltpu.make_async_copy(snd.at[s, me], ret.at[s, me], qloc.at[s]).wait()
        plane_copies(ret, s, qsend, qrecv).wait_recv()
        rows = ret[s].reshape(2 * TOK, HALF)
        return dot(comb[s, 0], rows) + dot(comb[s, 1], rows)

    def hop(buffer, k, device, n):
        copy = remote(buffer.at[k], buffer.at[k - 1], rsend.at[n, k], rrecv.at[n, k - 1], device)
        copy.start()
        sends.append(copy)

    def landed(buffer, k, n):
        remote(buffer.at[k], buffer.at[k], rsend.at[n, k], rrecv.at[n, k], ahead).wait_recv()

    def join(buffer, k, part, device, n):
        landed(buffer, k, n)
        buffer[k] = (buffer[k].astype(F32) + part).astype(BF16)
        hop(buffer, k, device, n)

    down(3)
    down(-3)
    experts_on(4)
    down(4)
    down(2)
    maj[4] = combined(4).astype(BF16)
    hop(maj, 4, ahead, 0)
    down(-2)
    part, minor = combined(3), combined(-3)
    mnr[3] = minor.astype(BF16)
    hop(mnr, 3, behind, 1)
    down(1)
    join(maj, 3, part, ahead, 0)
    down(-1)
    part, minor = combined(2), combined(-2)
    down(0)
    join(mnr, 2, minor, behind, 1)
    join(maj, 2, part, ahead, 0)
    part, minor = combined(1), combined(-1)
    half_rows = (pl.ds(0, 64), pl.ds(64, 64))

    def last(buffer, half, device, n):
        copy = remote(
            buffer.at[1, half_rows[half]], buffer.at[0, half_rows[half]], lsend.at[n, half], lrecv.at[n, half], device
        )
        copy.start()
        sends.append(copy)

    landed(mnr, 1, 1)
    landed(maj, 1, 0)
    for half, rows in enumerate(half_rows):
        for n, (buffer, more, device) in enumerate(((maj, part, ahead), (mnr, minor, behind))):
            buffer[1, rows] = (buffer[1, rows].astype(F32) + more[64 * half : 64 * half + 64]).astype(BF16)
            last(buffer, half, device, n)
    part = combined(0)

    def pass_y(owner, half, step, n):
        ref = sall.at[owner, half_rows[half]]
        copy = remote(ref, ref, xsend.at[n, half], xrecv.at[n, half], along_y(step))
        copy.start()
        sends.append(copy)

    def got_y(owner, half, n):
        ref = sall.at[owner, half_rows[half]]
        remote(ref, ref, xsend.at[n, half], xrecv.at[n, half], core).wait_recv()

    below, above, across_y = (y4 + 3) % 4, (y4 + 1) % 4, (y4 + 2) % 4
    for half, rows in enumerate(half_rows):
        total = part[64 * half : 64 * half + 64]
        for n, buffer in enumerate((maj, mnr)):
            ref = buffer.at[0, rows]
            remote(ref, ref, lsend.at[n, half], lrecv.at[n, half], ahead).wait_recv()
            total = total + buffer[0, rows].astype(F32)
        sall[y4, rows] = total.astype(BF16)
        pass_y(y4, half, 1, 0)
        pass_y(y4, half, 3, 1)
    got_y(below, 0, 0)
    pass_y(below, 0, 1, 2)
    got_y(above, 1, 1)
    pass_y(above, 1, 3, 2)
    got_y(below, 1, 0)
    got_y(above, 0, 1)
    swaps = []
    for half, rows in enumerate(half_rows):
        got_y(across_y, half, 2)
        for q in range(2):
            feature = jnp.concatenate([sall[q, rows].astype(F32), sall[q + 2, rows].astype(F32)], axis=1)
            mean_square = jnp.sum(feature * feature, axis=1, keepdims=True) / D
            nall[c, q, rows] = (feature * lax.rsqrt(mean_square + 1e-05) * gain[...].reshape(1, D)).astype(BF16)
        ref = nall.at[c, :, rows]
        swap = remote(ref, ref, nsend.at[half], nrecv.at[half], core)
        swap.start()
        swaps.append(swap)
    lanes = pl.ds(pl.multiple_of(group * UNITS, 128), UNITS)

    def predict(core_of):
        return lax.dot_general(
            nall[core_of].reshape(256, D), wall[...].reshape(256, D), (((1,), (1,)), ((), ())),
            preferred_element_type=F32,
        )

    own_part = predict(c)
    for swap in swaps:
        swap.wait()
    follow = remote(nall.at[0, :, pl.ds(0, 16), lanes], first, fsem.at[0], fsem.at[1], before)
    follow.start()
    other_part = predict(1 - c)
    feature, column = iota((UNITS, 256), 0), iota((UNITS, 256), 1)
    x_of, z_of, i_of = (column // 8) % 4, column // 32, column % 8
    choose = ((feature == y * 384 + z_of * 48 + x_of * 12 + c * 6 + i_of) & (i_of < 6)).astype(F32).astype(BF16)
    follow.wait()
    row = iota((TOK, 1), 0)
    last_chip = chip == 31
    quad = y * 2 + c
    for core_of, predicted in ((c, own_part), (1 - c, other_part)):
        for y_of in range(2):
            own = nall[core_of, y_of, :, lanes].astype(F32)
            beside_row = nall[1, y_of, 0:16, lanes].astype(F32)[0:1, :]
            beyond = jnp.where(last_chip, first[1 - y_of].astype(F32)[0:1, :], first[y_of].astype(F32)[0:1, :])
            following = jnp.where(core_of == 0, beside_row, beyond)
            target = jnp.where(row == TOK - 1, following, pltpu.roll(own, TOK - 1, 0)).astype(BF16)
            residual = predicted[y_of * TOK : y_of * TOK + TOK] - dot(target, choose)
            position = wide_of(y_of, z, x, core_of) * TOK + row
            err[y_of * 2 + core_of] = jnp.where(position < 128 * TOK - 1, residual, 0.0).astype(BF16)
    keep_err = pltpu.make_async_copy(err.at[quad], eall.at[quad], dloc.at[0])
    keep_err.start()

    def send_err(j, carry):
        n = (quad + j) % 4
        remote(
            err.at[n], eall.at[quad], esem.at[0], esem.at[1], (group, wide_of(n // 2, z, x, n % 2))
        ).start()
        return carry

    lax.fori_loop(1, 4, send_err, 0)

    before_order, after_order = iota((256, 192), 0), iota((256, 192), 1)
    matched = before_order == (after_order // 6 % 4) * 8 + (after_order // 24) * 32 + after_order % 6
    compact = matched.astype(F32).astype(BF16)
    factors = []
    for core_of in range(2):
        for y_of in range(2):
            factors.append(dot(err[y_of * 2 + core_of], compact).T)
    factors = jnp.concatenate(factors, axis=1).astype(BF16)
    gsum[...] = dot(factors, nall[...].reshape(512, D)) * grad_scale

    def own_part(d):
        s = (z + 8 + d * sigma) % 8
        return gsum[pl.ds(pl.multiple_of(24 * s, 8), 24), :].reshape(3, SLOT, D)

    def ghop(buffer, k, device, n):
        copy = remote(buffer.at[k], buffer.at[k - 1], gsend.at[n, k], grecv.at[n, k - 1], device)
        copy.start()
        sends.append(copy)

    def glanded(buffer, k, n):
        remote(buffer.at[k], buffer.at[k], gsend.at[n, k], grecv.at[n, k], ahead).wait_recv()

    gmaj[4] = own_part(4).astype(BF16)
    ghop(gmaj, 4, ahead, 0)
    gmnr[3] = own_part(-3).astype(BF16)
    ghop(gmnr, 3, behind, 1)

    keep_err.wait()
    others = remote(err.at[pl.ds(0, 3)], eall.at[pl.ds(0, 3)], esem.at[0], esem.at[1], core)
    others.wait()
    mixed, where_to = iota((1024, UNITS), 0), iota((1024, UNITS), 1)
    i_of, x_of, z_of, n_of = mixed % 8, (mixed // 8) % 4, (mixed // 32) % 8, mixed // 256
    matched = where_to == (n_of // 2) * 384 + z_of * 48 + x_of * 12 + (n_of % 2) * 6 + i_of
    restore = (matched & (i_of < 6)).astype(F32).astype(BF16)
    every = jnp.concatenate([eall[n] for n in range(4)], axis=1)
    error_ref[...] = dot(every, restore).astype(BF16)

    for k in (3, 2, 1):
        glanded(gmaj, k, 0)
        gmaj[k] = (gmaj[k].astype(F32) + own_part(k)).astype(BF16)
        ghop(gmaj, k, ahead, 0)
        if k < 3:
            glanded(gmnr, k, 1)
            gmnr[k] = (gmnr[k].astype(F32) + own_part(-k)).astype(BF16)
            ghop(gmnr, k, behind, 1)
    glanded(gmnr, 0, 1)
    glanded(gmaj, 0, 0)
    total = own_part(0) + gmnr[0].astype(F32) + gmaj[0].astype(F32)
    total = total.reshape(24, D).astype(BF16)
    q, r = iota((32, 24), 0), iota((32, 24), 1)
    expand = ((q // 8) * 6 + q % 8 == r) & (q % 8 < 6)
    pieces[...] = dot(expand.astype(F32).astype(BF16), total).reshape(4, SLOT, D).astype(BF16)
    keep_fin = pltpu.make_async_copy(pieces.at[x], fin.at[x], dloc.at[1])
    keep_fin.start()

    def send(j, carry):
        n = (x + j) % 4
        remote(pieces.at[n], fin.at[x], fsend, frecv, (group, wide_of(y, z, n, c))).start()
        return carry

    lax.fori_loop(1, 4, send, 0)
    keep_fin.wait()
    whole = remote(pieces.at[pl.ds(0, 3)], fin.at[pl.ds(0, 3)], fsend, frecv, core)
    whole.wait_recv()
    grad_ref[...] = jnp.sum(fin[...].astype(F32), axis=0).astype(BF16)
    whole.wait_send()
    for copy in sends:
        copy.wait_send()
    for s in range(NZ):
        plane_copies(ret, s, qsend, qrecv).wait_send()


def params(number=None):
    if number is None:
        return pltpu.CompilerParams(vmem_limit_bytes=62 << 20)
    return pltpu.CompilerParams(vmem_limit_bytes=62 << 20, collective_id=number, has_side_effects=True)


VM = pl.BlockSpec(memory_space=pltpu.VMEM)
ANY = pl.BlockSpec(memory_space=pl.ANY)


def out(shape, kind=BF16):
    return jax.ShapeDtypeStruct(shape, kind)


def shards(
    tokens, routes, router, gate_codes, gate_scales, up_codes, up_scales, down_codes, down_scales, norm_gain,
    drafter_weight,
):
    dma = pltpu.SemaphoreType.DMA
    frame = (NZ, PLANE, SLOT, HALF)
    double = (NZ, ALL, SLOT, HALF)
    grad_scale = 1.0 / math.sqrt(TOK * lax.axis_size("wide"))
    error, gradient = pl.pallas_call(
        functools.partial(layer_kernel, grad_scale),
        out_shape=(out((TOK, UNITS)), out((SLOT, D))),
        in_specs=[ANY] * 3 + [VM] * 2 + [ANY] * 6,
        out_specs=(VM, VM),
        scratch_shapes=[
            pltpu.VMEM((D, TOK), BF16),
            pltpu.VMEM((4, TOK), jnp.int32),
            pltpu.VMEM((D, TOK), BF16),
            pltpu.VMEM(frame, BF16),
            pltpu.VMEM(double, BF16),
            pltpu.VMEM(double, BF16),
            pltpu.VMEM(double, BF16),
            pltpu.VMEM((WORDS, UNITS), jnp.int32),
            pltpu.VMEM((90, 1, UNITS), jnp.int32),
            pltpu.VMEM((D, 256), jnp.int32),
            pltpu.VMEM((24, D), jnp.int32),
            pltpu.VMEM((2, 24, HALF), jnp.int32),
            pltpu.VMEM((D, UNITS), BF16),
            pltpu.VMEM((D, UNITS), BF16),
            pltpu.VMEM((2, UNITS, HALF), BF16),
            pltpu.VMEM((NZ, 2, TOK, 2 * TOK), BF16),
            pltpu.VMEM((NZ, SLOT, 12 * TOK), BF16),
            pltpu.VMEM((SLOT, D), BF16),
            pltpu.VMEM((1024, UNITS), BF16),
            pltpu.VMEM((5, TOK, HALF), BF16),
            pltpu.VMEM((4, TOK, HALF), BF16),
            pltpu.VMEM((4, TOK, HALF), BF16),
            dma((3,)), dma((6,)), dma((7, 3)), dma((7, 3)), dma((NZ,)), dma((NZ,)), dma((NZ,)),
            dma((NZ,)), dma((NZ,)), dma((NZ,)), dma((2, 5)), dma((2, 5)), dma((2, 2)), dma((2, 2)), dma((3, 2)), dma((3, 2)),
            dma, dma, dma,
            pltpu.VMEM((NZ, 4, SLOT, D), BF16),
            pltpu.VMEM((2, 2, TOK, D), BF16),
            pltpu.VMEM((2, 16, UNITS), BF16),
            pltpu.VMEM((4, TOK, 256), BF16),
            pltpu.VMEM((4, TOK, 256), BF16),
            pltpu.VMEM((192, D), F32),
            pltpu.VMEM((5, 3, SLOT, D), BF16),
            pltpu.VMEM((4, 3, SLOT, D), BF16),
            pltpu.VMEM((4, SLOT, D), BF16),
            pltpu.VMEM((4, SLOT, D), BF16),
            dma((2,)), dma((2,)), dma((2,)), dma((2,)), dma((2, 5)), dma((2, 5)), dma, dma, dma((2,)),
        ],
        compiler_params=params(1),
        name="layer",
    )(
        tokens.T, routes.T, router, drafter_weight, norm_gain, gate_codes[0],
        gate_scales.transpose(1, 0, 2), up_codes[0], up_scales.transpose(1, 0, 2),
        down_codes[0].T, down_scales[0],
    )
    return (error, gradient[:6])


def solution(mesh):
    placed = (
        P("wide", None),
        P("wide", None),
        P(),
        P("wide", None, "group"),
        P("wide", None, "group"),
        P("wide", None, "group"),
        P("wide", None, "group"),
        P("wide", "group", None),
        P("wide", "group", None),
        P(),
        P(("group", "wide"), None),
    )
    return jax.shard_map(
        shards,
        mesh=mesh,
        in_specs=placed,
        out_specs=(P("wide", "group"), P(("group", "wide"), None)),
        check_vma=False,
    )
```

```python
import functools
import math

import jax
import jax.numpy as jnp
from jax import lax
from jax.experimental import pallas as pl
from jax.experimental.pallas import tpu as pltpu
from jax.sharding import PartitionSpec as P

MESH = pl.DeviceIdType.MESH
F32 = jnp.float32
BF16 = jnp.bfloat16

D = 2880
TOK = 128
NZ = 8
PLANE = 16
SLOT = 8
SLABS = TOK // SLOT
HALF = D // 2
ALL = 2 * PLANE
UNITS = 768
WORDS = 960


def place():
    group, wide = lax.axis_index("group"), lax.axis_index("wide")
    y, z, x, c = wide // 64, (wide // 8) % 8, (wide // 2) % 4, wide % 2
    return group, wide, y, z, x, c


def wide_of(y, z, x, c):
    return y * 64 + z * 8 + x * 2 + c


def plane_wide(p, z):
    return (p // 8) * 64 + z * 8 + p % 8


def iota(shape, dim, kind=jnp.int32):
    return lax.broadcasted_iota(jnp.int32, shape, dim).astype(kind)


def dot(a, b):
    return jnp.dot(a, b, preferred_element_type=F32)


def dot_first(a, b):
    return lax.dot_general(a, b, (((0,), (0,)), ((), ())), preferred_element_type=F32)


def remote(src, dst, send, recv, device):
    return pltpu.make_async_remote_copy(
        src_ref=src, dst_ref=dst, send_sem=send, recv_sem=recv, device_id=device, device_id_type=MESH
    )


def spread(columns):
    parts = []
    for start, length in [(0, 384), (384, 384), (768, 384), (1152, 288)]:
        third = length // 3
        row = iota((length, length), 0)
        column = iota((length, length), 1)
        order = (row == 3 * (column % third) + column // third).astype(F32).astype(BF16)
        parts.append(dot_first(columns[start : start + length, :], order).astype(BF16))
    return parts


def level(nibble):
    m = nibble & 7
    twice = m + jnp.maximum(m - 4, 0) + 2 * jnp.maximum(m - 6, 0)
    return twice.astype(F32)


def unpack(words, j, scales):
    nibble = (words >> (4 * j)) & 15
    half = jnp.exp2((scales - 1).astype(F32))
    return level(nibble) * jnp.where(nibble >= 8, -half, half)


def scale_rows(ref, q, j, width):
    r = iota((32, width), 0)
    block = (3 * r + j) // 32
    rows = [ref[3 * q + n] for n in range(3)]
    return jnp.where(block == 0, rows[0], jnp.where(block == 1, rows[1], rows[2]))


def dequant_in(codes, scales, out, q, base, third):
    words = codes[pl.ds(pl.multiple_of(32 * q, 32), 32), :]
    for j in range(3):
        values = unpack(words, j, scale_rows(scales, q, j, words.shape[1]))
        out[pl.ds(pl.multiple_of(base + third * j, 32), 32), :] = values.astype(BF16)


def dequant_wide(codes, scales, out, half):
    def step(n, carry):
        dequant_in(codes, scales, out, 15 * half + n, HALF * half + (n // 4) * 384 + (n % 4) * 32, 128)
        return carry

    lax.fori_loop(0, 12, step, 0)
    for n in range(3):
        dequant_in(codes, scales, out, 15 * half + 12 + n, HALF * half + 1152 + 32 * n, 96)


def layer_kernel(
    grad_scale, tokens_ref, routes_ref, router_ref, drafter_ref, gain, gc, gs, uc, us, dc, ds, error_ref, grad_ref,
    tokv, routev, routerv, agb, snd, xr, ret, wide_codes, wide_scales, dcv, dsv, dsh, wg, wu, wd, comb, metas, slab, hid,
    maj, mnr, sall, in_sem, code_sem, zsend, zrecv, psend, precv, loc, qsend, qrecv, qloc,
    rsend, rrecv, lsend, lrecv, xsend, xrecv, wsend, wrecv, wloc,
    wall, nall, first, err, eall, gsum, gmaj, gmnr, pieces, fin, fsem, nsend, nrecv, esem, gsend, grecv, fsend, frecv, dloc,
):
    group, wide, y, z, x, c = place()
    me = group * PLANE + y * 8 + x * 2 + c
    sigma = 1 - 2 * c
    y4 = 2 * group + y

    def along_y(n):
        place_y = (y4 + n) % 4
        return (place_y // 2, wide_of(place_y % 2, z, x, c))

    core = (group, wide_of(y, z, x, 1 - c))
    right = (group, wide_of(y, (z + 1) % 8, x, c))
    left = (group, wide_of(y, (z + 7) % 8, x, c))
    ahead = (group, wide_of(y, (z + 8 + sigma) % 8, x, c))
    behind = (group, wide_of(y, (z + 8 - sigma) % 8, x, c))

    loads = [
        pltpu.make_async_copy(a, b, in_sem.at[n])
        for n, (a, b) in enumerate([(tokens_ref, tokv), (routes_ref, routev), (router_ref, routerv)])
    ]
    gate_codes = pltpu.make_async_copy(gc, wide_codes, code_sem.at[0])
    gate_scales = pltpu.make_async_copy(gs, wide_scales, code_sem.at[1])
    up_codes = pltpu.make_async_copy(uc, wide_codes, code_sem.at[2])
    up_scales = pltpu.make_async_copy(us, wide_scales, code_sem.at[3])
    down_codes = pltpu.make_async_copy(dc, dcv, code_sem.at[4])
    down_scales = pltpu.make_async_copy(ds, dsv, code_sem.at[5])
    for copy in loads + [gate_codes, gate_scales, down_codes, down_scales]:
        copy.start()

    barrier = pltpu.get_barrier_semaphore()
    chip = z * 4 + x
    before, after = (chip + 31) % 32, (chip + 1) % 32
    before = (group, wide_of(y, before // 4, before % 4, c))
    after = (group, wide_of(y, after // 4, after % 4, c))
    for neighbour in (left, right, before, after):
        pl.semaphore_signal(barrier, inc=1, device_id=neighbour, device_id_type=MESH)

    def plane_device(n):
        return (n // PLANE, plane_wide(n % PLANE, z))

    def greet(j, carry):
        pl.semaphore_signal(barrier, inc=1, device_id=plane_device((me + j) % ALL), device_id_type=MESH)
        return carry

    lax.fori_loop(1, ALL, greet, 0)

    for copy in loads:
        copy.wait()
    columns = tokv[...]
    column = 0
    for part in spread(tokv[pl.ds(pl.multiple_of(HALF * group, 16), HALF), :]):
        width = part.shape[1]
        agb[z, :, :, column : column + width] = part.astype(F32).reshape(SLABS, SLOT, width).astype(BF16)
        column += width
    weight = jax.nn.sigmoid(dot_first(routerv[...], columns))
    named_expert = iota((TOK, TOK), 0)
    routes, high, low = [], [], []
    for k in range(4):
        route = routev[k : k + 1, :]
        chosen = jnp.sum(jnp.where(named_expert == route, weight, 0.0), axis=0, keepdims=True)
        top = chosen.astype(BF16).astype(F32)
        routes.append(route.astype(F32))
        high.append(top)
        low.append(chosen - top)
    line = jnp.concatenate(routes + high + low, axis=1)
    metas[z] = jnp.broadcast_to(line, (SLOT, 12 * TOK)).astype(BF16)
    slab[...] = jnp.concatenate([drafter_ref[...].astype(F32), jnp.zeros((2, D), F32)], axis=0).astype(BF16)
    pl.semaphore_wait(barrier, 35)

    sends = []
    def pass_z(ref, device, n, part):
        copy = remote(ref, ref, zsend.at[n, part], zrecv.at[n, part], device)
        copy.start()
        sends.append(copy)

    def forward(s, device, n):
        pass_z(metas.at[s], device, n, 0)
        pass_z(agb.at[s], device, n, 1)

    def got_z(ref, n, part):
        remote(ref, ref, zsend.at[n, part], zrecv.at[n, part], right).wait_recv()

    def arrived(s, n):
        got_z(metas.at[s], n, 0)
        got_z(agb.at[s], n, 1)

    upper = (iota((TOK, TOK), 0) < iota((TOK, TOK), 1)).astype(F32).astype(BF16)
    p_rows = iota((PLANE, 1), 0)
    experts = ((p_rows // 8) * 64 + z * 8 + p_rows % 8).astype(F32)

    def plane_send(start, source, target, s, send_sem, recv_sem):
        def send(j, carry):
            n = (me + j) % ALL
            remote(
                source.at[s, n % start], target.at[s, me], send_sem.at[s], recv_sem.at[s], plane_device(n)
            ).start()
            return carry

        lax.fori_loop(1, ALL, send, 0)

    def plane_copies(target, s, send_sem, recv_sem):
        ref = target.at[s, pl.ds(0, ALL - 1)]
        return remote(ref, ref, send_sem.at[s], recv_sem.at[s], core)

    def relay(s):
        meta = metas[s].astype(F32)[0:1, :]
        named = jnp.zeros((PLANE, TOK), F32)
        weight = jnp.zeros((PLANE, TOK), F32)
        for k in range(4):
            hit = (experts == meta[:, k * TOK : (k + 1) * TOK]).astype(F32)
            value = meta[:, (4 + k) * TOK : (5 + k) * TOK] + meta[:, (8 + k) * TOK : (9 + k) * TOK]
            named = named + hit
            weight = weight + hit * value
        rank = dot(named.astype(BF16), upper)
        slot = iota((PLANE, SLOT, TOK), 1, F32)
        pick = jnp.where(rank[:, None, :] == slot, named[:, None, :], 0.0)
        rows = dot(pick.reshape(TOK, TOK).astype(BF16), agb[s].reshape(TOK, HALF))
        snd[s, 0:PLANE] = rows.reshape(PLANE, SLOT, HALF).astype(BF16)
        pltpu.make_async_copy(snd.at[s, me % PLANE], xr.at[s, me], loc.at[s]).start()
        plane_send(PLANE, snd, xr, s, psend, precv)
        weighted = (pick * weight[:, None, :]).reshape(TOK, TOK).T
        weighted = jnp.concatenate([weighted, weighted], axis=1)
        top = weighted.astype(BF16)
        comb[s, 0] = top
        comb[s, 1] = (weighted - top.astype(F32)).astype(BF16)

    def source(d):
        return (z + 8 + d * sigma) % 8

    order_row = iota((UNITS, UNITS), 0)
    order_column = iota((UNITS, UNITS), 1)

    def experts_on(*distances):
        lower, upper_half = [], []
        for d in distances:
            s = source(d)
            pltpu.make_async_copy(snd.at[s, 0], xr.at[s, 0], loc.at[s]).wait()
            plane_copies(xr, s, psend, precv).wait_recv()
            lower.append(xr[s, 0:PLANE].reshape(TOK, HALF))
            upper_half.append(xr[s, PLANE:ALL].reshape(TOK, HALF))
        lower = jnp.concatenate(lower, axis=0)
        upper_half = jnp.concatenate(upper_half, axis=0)
        gate = dot(lower, wg[0:HALF]) + dot(upper_half, wg[HALF:D])
        act = (jax.nn.silu(gate) * (dot(lower, wu[0:HALF]) + dot(upper_half, wu[HALF:D]))).astype(BF16)
        order = (order_row == 3 * (order_column % 256) + order_column // 256).astype(F32).astype(BF16)
        act = dot(act, order).astype(BF16)
        for n, d in enumerate(distances):
            hid[pl.ds(pl.multiple_of(TOK * source(d), TOK), TOK), :] = act[n * TOK : (n + 1) * TOK]

    def dequant_down(half):
        def block(start, width):
            columns = dcv[pl.ds(pl.multiple_of(HALF * half + start, 32), width), :].T
            lanes = pl.ds(start if width < 128 else pl.multiple_of(start, 128), width)
            for q in range(8):
                for j in range(3):
                    r = iota((32, width), 0)
                    unit = (3 * r + j) // 32
                    rows = [dsh[half, 3 * q + n : 3 * q + n + 1, lanes] for n in range(3)]
                    scales = jnp.where(unit == 0, rows[0], jnp.where(unit == 1, rows[1], rows[2]))
                    values = unpack(columns[32 * q : 32 * q + 32], j, scales)
                    wd[half, 256 * j + 32 * q : 256 * j + 32 * q + 32, lanes] = values.astype(BF16)

        def step(n, carry):
            block(128 * n, 128)
            return carry

        lax.fori_loop(0, 11, step, 0)
        block(1408, 32)

    def beside(n):
        if n == 0:
            gate_codes.wait()
            gate_scales.wait()
            dequant_wide(wide_codes, wide_scales, wg, 0)
        elif n == 1:
            dequant_wide(wide_codes, wide_scales, wg, 1)
            up_codes.start()
            up_scales.start()
        elif n == 2:
            down_codes.wait()
            down_scales.wait()
            for half in range(2):
                dsh[half] = dsv[:, HALF * half : HALF * half + HALF]
            dequant_down(0)
        elif n == 3:
            up_codes.wait()
            up_scales.wait()
            dequant_wide(wide_codes, wide_scales, wu, 0)
        elif n == 4:
            dequant_wide(wide_codes, wide_scales, wu, 1)
        elif n == 5:
            dequant_down(1)

    keep = pltpu.make_async_copy(slab, wall.at[z, x], wloc)
    keep.start()

    def share_x(j, carry):
        remote(slab, wall.at[z, x], wsend, wrecv, (group, wide_of(y, z, (x + j) % 4, c))).start()
        return carry

    lax.fori_loop(1, 4, share_x, 0)
    three = remote(wall.at[z, pl.ds(0, 3)], wall.at[z, pl.ds(0, 3)], wsend, wrecv, core)
    forward(z, right, 0)
    forward(z, left, 1)
    relay(z)
    keep.wait()
    three.wait()
    pass_z(wall.at[z], right, 0, 2)
    pass_z(wall.at[z], left, 1, 2)
    for k in (1, 2, 3):
        beside(k - 1)
        back, front = (z + 8 - k) % 8, (z + k) % 8
        arrived(back, 2 * k - 2)
        if k < 3:
            forward(back, right, 2 * k)
        arrived(front, 2 * k - 1)
        if k < 3:
            forward(front, left, 2 * k + 1)
        else:
            forward((z + 8 - 3 * sigma) % 8, ahead, 6)
        relay(back)
        relay(front)
        got_z(wall.at[back], 2 * k - 2, 2)
        if k < 3:
            pass_z(wall.at[back], right, 2 * k, 2)
        got_z(wall.at[front], 2 * k - 1, 2)
        if k < 3:
            pass_z(wall.at[front], left, 2 * k + 1, 2)
        else:
            pass_z(wall.at[(z + 8 - 3 * sigma) % 8], ahead, 6, 2)
    beside(3)
    opposite = (z + 4) % 8
    arrived(opposite, 6)
    relay(opposite)
    got_z(wall.at[opposite], 6, 2)
    beside(4)
    def down(d):
        s = source(d)
        plane_copies(xr, s, psend, precv).wait_send()
        acts = hid[pl.ds(pl.multiple_of(TOK * s, TOK), TOK), :]
        for half in range(2):
            rows = dot(acts, wd[half])
            snd[s, PLANE * half : PLANE * half + PLANE] = rows.reshape(PLANE, SLOT, HALF).astype(BF16)
        pltpu.make_async_copy(snd.at[s, me], ret.at[s, me], qloc.at[s]).start()
        plane_send(ALL, snd, ret, s, qsend, qrecv)

    experts_on(0, 1)
    beside(5)
    experts_on(-1, 2)
    experts_on(-2, 3)
    down(3)
    experts_on(-3)

    def combined(d):
        s = source(d)
        pltpu.make_async_copy(snd.at[s, me], ret.at[s, me], qloc.at[s]).wait()
        plane_copies(ret, s, qsend, qrecv).wait_recv()
        rows = ret[s].reshape(2 * TOK, HALF)
        return dot(comb[s, 0], rows) + dot(comb[s, 1], rows)

    def hop(buffer, k, device, n):
        copy = remote(buffer.at[k], buffer.at[k - 1], rsend.at[n, k], rrecv.at[n, k - 1], device)
        copy.start()
        sends.append(copy)

    def landed(buffer, k, n):
        remote(buffer.at[k], buffer.at[k], rsend.at[n, k], rrecv.at[n, k], ahead).wait_recv()

    def join(buffer, k, part, device, n):
        landed(buffer, k, n)
        buffer[k] = (buffer[k].astype(F32) + part).astype(BF16)
        hop(buffer, k, device, n)

    experts_on(4)
    down(4)
    down(-3)
    down(2)
    maj[4] = combined(4).astype(BF16)
    hop(maj, 4, ahead, 0)
    down(-2)
    part, minor = combined(3), combined(-3)
    mnr[3] = minor.astype(BF16)
    hop(mnr, 3, behind, 1)
    down(1)
    join(maj, 3, part, ahead, 0)
    down(-1)
    part, minor = combined(2), combined(-2)
    down(0)
    join(mnr, 2, minor, behind, 1)
    join(maj, 2, part, ahead, 0)
    part, minor = combined(1), combined(-1)
    half_rows = (pl.ds(0, 64), pl.ds(64, 64))

    def last(buffer, half, device, n):
        copy = remote(
            buffer.at[1, half_rows[half]], buffer.at[0, half_rows[half]], lsend.at[n, half], lrecv.at[n, half], device
        )
        copy.start()
        sends.append(copy)

    landed(mnr, 1, 1)
    landed(maj, 1, 0)
    for half, rows in enumerate(half_rows):
        for n, (buffer, more, device) in enumerate(((maj, part, ahead), (mnr, minor, behind))):
            buffer[1, rows] = (buffer[1, rows].astype(F32) + more[64 * half : 64 * half + 64]).astype(BF16)
            last(buffer, half, device, n)
    part = combined(0)

    def pass_y(owner, half, step, n):
        ref = sall.at[owner, half_rows[half]]
        copy = remote(ref, ref, xsend.at[n, half], xrecv.at[n, half], along_y(step))
        copy.start()
        sends.append(copy)

    def got_y(owner, half, n):
        ref = sall.at[owner, half_rows[half]]
        remote(ref, ref, xsend.at[n, half], xrecv.at[n, half], core).wait_recv()

    below, above, across_y = (y4 + 3) % 4, (y4 + 1) % 4, (y4 + 2) % 4
    for half, rows in enumerate(half_rows):
        total = part[64 * half : 64 * half + 64]
        for n, buffer in enumerate((maj, mnr)):
            ref = buffer.at[0, rows]
            remote(ref, ref, lsend.at[n, half], lrecv.at[n, half], ahead).wait_recv()
            total = total + buffer[0, rows].astype(F32)
        sall[y4, rows] = total.astype(BF16)
        pass_y(y4, half, 1, 0)
        pass_y(y4, half, 3, 1)
    got_y(below, 0, 0)
    pass_y(below, 0, 1, 2)
    got_y(above, 1, 1)
    pass_y(above, 1, 3, 2)
    got_y(below, 1, 0)
    got_y(above, 0, 1)
    swaps = []
    for half, rows in enumerate(half_rows):
        got_y(across_y, half, 2)
        for q in range(2):
            feature = jnp.concatenate([sall[q, rows].astype(F32), sall[q + 2, rows].astype(F32)], axis=1)
            mean_square = jnp.sum(feature * feature, axis=1, keepdims=True) / D
            nall[c, q, rows] = (feature * lax.rsqrt(mean_square + 1e-05) * gain[...].reshape(1, D)).astype(BF16)
        ref = nall.at[c, :, rows]
        swap = remote(ref, ref, nsend.at[half], nrecv.at[half], core)
        swap.start()
        swaps.append(swap)
    lanes = pl.ds(pl.multiple_of(group * UNITS, 128), UNITS)

    def predict(core_of):
        return lax.dot_general(
            nall[core_of].reshape(256, D), wall[...].reshape(256, D), (((1,), (1,)), ((), ())),
            preferred_element_type=F32,
        )

    own_part = predict(c)
    for swap in swaps:
        swap.wait()
    follow = remote(nall.at[0, :, pl.ds(0, 16), lanes], first, fsem.at[0], fsem.at[1], before)
    follow.start()
    other_part = predict(1 - c)
    feature, column = iota((UNITS, 256), 0), iota((UNITS, 256), 1)
    x_of, z_of, i_of = (column // 8) % 4, column // 32, column % 8
    choose = ((feature == y * 384 + z_of * 48 + x_of * 12 + c * 6 + i_of) & (i_of < 6)).astype(F32).astype(BF16)
    follow.wait()
    row = iota((TOK, 1), 0)
    last_chip = chip == 31
    quad = y * 2 + c
    for core_of, predicted in ((c, own_part), (1 - c, other_part)):
        for y_of in range(2):
            own = nall[core_of, y_of, :, lanes].astype(F32)
            beside_row = nall[1, y_of, 0:16, lanes].astype(F32)[0:1, :]
            beyond = jnp.where(last_chip, first[1 - y_of].astype(F32)[0:1, :], first[y_of].astype(F32)[0:1, :])
            following = jnp.where(core_of == 0, beside_row, beyond)
            target = jnp.where(row == TOK - 1, following, pltpu.roll(own, TOK - 1, 0)).astype(BF16)
            residual = predicted[y_of * TOK : y_of * TOK + TOK] - dot(target, choose)
            position = wide_of(y_of, z, x, core_of) * TOK + row
            err[y_of * 2 + core_of] = jnp.where(position < 128 * TOK - 1, residual, 0.0).astype(BF16)
    keep_err = pltpu.make_async_copy(err.at[quad], eall.at[quad], dloc.at[0])
    keep_err.start()

    def send_err(j, carry):
        n = (quad + j) % 4
        remote(
            err.at[n], eall.at[quad], esem.at[0], esem.at[1], (group, wide_of(n // 2, z, x, n % 2))
        ).start()
        return carry

    lax.fori_loop(1, 4, send_err, 0)

    before_order, after_order = iota((256, 192), 0), iota((256, 192), 1)
    matched = before_order == (after_order // 6 % 4) * 8 + (after_order // 24) * 32 + after_order % 6
    compact = matched.astype(F32).astype(BF16)
    factors = []
    for core_of in range(2):
        for y_of in range(2):
            factors.append(dot(err[y_of * 2 + core_of], compact).T)
    factors = jnp.concatenate(factors, axis=1).astype(BF16)
    gsum[...] = dot(factors, nall[...].reshape(512, D)) * grad_scale

    def own_part(d):
        s = (z + 8 + d * sigma) % 8
        return gsum[pl.ds(pl.multiple_of(24 * s, 8), 24), :].reshape(3, SLOT, D)

    def ghop(buffer, k, device, n):
        copy = remote(buffer.at[k], buffer.at[k - 1], gsend.at[n, k], grecv.at[n, k - 1], device)
        copy.start()
        sends.append(copy)

    def glanded(buffer, k, n):
        remote(buffer.at[k], buffer.at[k], gsend.at[n, k], grecv.at[n, k], ahead).wait_recv()

    gmaj[4] = own_part(4).astype(BF16)
    ghop(gmaj, 4, ahead, 0)
    gmnr[3] = own_part(-3).astype(BF16)
    ghop(gmnr, 3, behind, 1)

    keep_err.wait()
    others = remote(err.at[pl.ds(0, 3)], eall.at[pl.ds(0, 3)], esem.at[0], esem.at[1], core)
    others.wait()
    mixed, where_to = iota((1024, UNITS), 0), iota((1024, UNITS), 1)
    i_of, x_of, z_of, n_of = mixed % 8, (mixed // 8) % 4, (mixed // 32) % 8, mixed // 256
    matched = where_to == (n_of // 2) * 384 + z_of * 48 + x_of * 12 + (n_of % 2) * 6 + i_of
    restore = (matched & (i_of < 6)).astype(F32).astype(BF16)
    every = jnp.concatenate([eall[n] for n in range(4)], axis=1)
    error_ref[...] = dot(every, restore).astype(BF16)

    for k in (3, 2, 1):
        glanded(gmaj, k, 0)
        gmaj[k] = (gmaj[k].astype(F32) + own_part(k)).astype(BF16)
        ghop(gmaj, k, ahead, 0)
        if k < 3:
            glanded(gmnr, k, 1)
            gmnr[k] = (gmnr[k].astype(F32) + own_part(-k)).astype(BF16)
            ghop(gmnr, k, behind, 1)
    glanded(gmnr, 0, 1)
    glanded(gmaj, 0, 0)
    total = own_part(0) + gmnr[0].astype(F32) + gmaj[0].astype(F32)
    total = total.reshape(24, D).astype(BF16)
    q, r = iota((32, 24), 0), iota((32, 24), 1)
    expand = ((q // 8) * 6 + q % 8 == r) & (q % 8 < 6)
    pieces[...] = dot(expand.astype(F32).astype(BF16), total).reshape(4, SLOT, D).astype(BF16)
    keep_fin = pltpu.make_async_copy(pieces.at[x], fin.at[x], dloc.at[1])
    keep_fin.start()

    def send(j, carry):
        n = (x + j) % 4
        remote(pieces.at[n], fin.at[x], fsend, frecv, (group, wide_of(y, z, n, c))).start()
        return carry

    lax.fori_loop(1, 4, send, 0)
    keep_fin.wait()
    whole = remote(pieces.at[pl.ds(0, 3)], fin.at[pl.ds(0, 3)], fsend, frecv, core)
    whole.wait_recv()
    grad_ref[...] = jnp.sum(fin[...].astype(F32), axis=0).astype(BF16)
    whole.wait_send()
    for copy in sends:
        copy.wait_send()
    for s in range(NZ):
        plane_copies(ret, s, qsend, qrecv).wait_send()


def params(number=None):
    if number is None:
        return pltpu.CompilerParams(vmem_limit_bytes=62 << 20)
    return pltpu.CompilerParams(vmem_limit_bytes=62 << 20, collective_id=number, has_side_effects=True)


VM = pl.BlockSpec(memory_space=pltpu.VMEM)
ANY = pl.BlockSpec(memory_space=pl.ANY)


def out(shape, kind=BF16):
    return jax.ShapeDtypeStruct(shape, kind)


def shards(
    tokens, routes, router, gate_codes, gate_scales, up_codes, up_scales, down_codes, down_scales, norm_gain,
    drafter_weight,
):
    dma = pltpu.SemaphoreType.DMA
    frame = (NZ, PLANE, SLOT, HALF)
    double = (NZ, ALL, SLOT, HALF)
    grad_scale = 1.0 / math.sqrt(TOK * lax.axis_size("wide"))
    error, gradient = pl.pallas_call(
        functools.partial(layer_kernel, grad_scale),
        out_shape=(out((TOK, UNITS)), out((SLOT, D))),
        in_specs=[ANY] * 3 + [VM] * 2 + [ANY] * 6,
        out_specs=(VM, VM),
        scratch_shapes=[
            pltpu.VMEM((D, TOK), BF16),
            pltpu.VMEM((4, TOK), jnp.int32),
            pltpu.VMEM((D, TOK), BF16),
            pltpu.VMEM(frame, BF16),
            pltpu.VMEM(double, BF16),
            pltpu.VMEM(double, BF16),
            pltpu.VMEM(double, BF16),
            pltpu.VMEM((WORDS, UNITS), jnp.int32),
            pltpu.VMEM((90, 1, UNITS), jnp.int32),
            pltpu.VMEM((D, 256), jnp.int32),
            pltpu.VMEM((24, D), jnp.int32),
            pltpu.VMEM((2, 24, HALF), jnp.int32),
            pltpu.VMEM((D, UNITS), BF16),
            pltpu.VMEM((D, UNITS), BF16),
            pltpu.VMEM((2, UNITS, HALF), BF16),
            pltpu.VMEM((NZ, 2, TOK, 2 * TOK), BF16),
            pltpu.VMEM((NZ, SLOT, 12 * TOK), BF16),
            pltpu.VMEM((SLOT, D), BF16),
            pltpu.VMEM((1024, UNITS), BF16),
            pltpu.VMEM((5, TOK, HALF), BF16),
            pltpu.VMEM((4, TOK, HALF), BF16),
            pltpu.VMEM((4, TOK, HALF), BF16),
            dma((3,)), dma((6,)), dma((7, 3)), dma((7, 3)), dma((NZ,)), dma((NZ,)), dma((NZ,)),
            dma((NZ,)), dma((NZ,)), dma((NZ,)), dma((2, 5)), dma((2, 5)), dma((2, 2)), dma((2, 2)), dma((3, 2)), dma((3, 2)),
            dma, dma, dma,
            pltpu.VMEM((NZ, 4, SLOT, D), BF16),
            pltpu.VMEM((2, 2, TOK, D), BF16),
            pltpu.VMEM((2, 16, UNITS), BF16),
            pltpu.VMEM((4, TOK, 256), BF16),
            pltpu.VMEM((4, TOK, 256), BF16),
            pltpu.VMEM((192, D), F32),
            pltpu.VMEM((5, 3, SLOT, D), BF16),
            pltpu.VMEM((4, 3, SLOT, D), BF16),
            pltpu.VMEM((4, SLOT, D), BF16),
            pltpu.VMEM((4, SLOT, D), BF16),
            dma((2,)), dma((2,)), dma((2,)), dma((2,)), dma((2, 5)), dma((2, 5)), dma, dma, dma((2,)),
        ],
        compiler_params=params(1),
        name="layer",
    )(
        tokens.T, routes.T, router, drafter_weight, norm_gain, gate_codes[0],
        gate_scales.transpose(1, 0, 2), up_codes[0], up_scales.transpose(1, 0, 2),
        down_codes[0].T, down_scales[0],
    )
    return (error, gradient[:6])


def solution(mesh):
    placed = (
        P("wide", None),
        P("wide", None),
        P(),
        P("wide", None, "group"),
        P("wide", None, "group"),
        P("wide", None, "group"),
        P("wide", None, "group"),
        P("wide", "group", None),
        P("wide", "group", None),
        P(),
        P(("group", "wide"), None),
    )
    return jax.shard_map(
        shards,
        mesh=mesh,
        in_specs=placed,
        out_specs=(P("wide", "group"), P(("group", "wide"), None)),
        check_vma=False,
    )
```
